32 devices in a mesh: gx: 16 (over z, y, core), gy: 2 (over x).
Axes of the slice: x: 2, y: 2, z: 4, core: 2. Of those that a mesh axis runs over, the one named last changes fastest.
Arguments:
- pressure_prev: float32 [128, 64, 256], P('gx', 'gy'), may hold values from -6 to 6
- pressure_now: float32 [128, 64, 256], P('gx', 'gy'), may hold values from -6 to 6
- courant: float32 [128, 64, 256], P('gx', 'gy'), may hold values from 0.05 to 0.18
- perturbation: float32 [128, 64, 256], P('gx', 'gy'), may hold values from 0.005 to 0.04
- source_pos: int32 [3], replicated, may hold values from 0 to 63
- wavelet: float32 [8], replicated, may hold values from -8 to 8
- rec_cells: int32 [16, 2, 128], P('gx', 'gy'), may hold values from 0 to 65535
- observed: float32 [16, 2, 8, 128], P('gx', 'gy'), may hold values from -20 to 20
Outputs:
- pressure: float32 [128, 64, 256], P('gx', 'gy')
- tangent: float32 [128, 64, 256], P('gx', 'gy')
- predicted: float32 [16, 2, 8, 128], P('gx', 'gy')
- updated_model: float32 [128, 64, 256], P('gx', 'gy')
The draws below stay inside these ranges and needn't reach their ends.
Inputs may be any that keep to these rules, and one draw needn't show every extreme that they name: `rec_cells`: indices of cells inside the device's own block. `source_pos`: A cell inside the grid.
All inputs are finite; a program needn't handle non-finite values.
Results may differ from the reference program's by a relative error of at most 0.00002.
Values sent between devices are 32-bit elements; how exact they have to be, the bound alone decides.
No kernel may reach another device: no remote copies, remote signals or barrier semaphores. Data moves between devices by JAX's collectives and lax.ppermute only.
A program may use at most 64 MiB of HBM per device.

```python
import math
import jax
import jax.numpy as jnp
from jax import lax

CX = 8
CY = 32
CZ = 256
NT = 8
REC = 128
NX = 128
NY = 64
NZ = 256
N_GX = 16
N_GY = 2


def draw_observed(key, part):
    key = jax.random.fold_in(key, 5)
    rows = jnp.arange(N_GX, dtype=jnp.float32)
    scale = 1.0 + 2.0 * rows / max(N_GX - 1, 1)
    values = jax.random.normal(key, (N_GX, N_GY, NT, REC), jnp.float32) * scale[:, None, None, None]
    return jnp.clip(values, -20.0, 20.0).astype(jnp.float32)


def plant(array, key, smallest, high):
    extent = array.shape
    spot = [jax.random.randint(jax.random.fold_in(key, axis), (), 0, extent[axis]) for axis in range(len(extent))]
    array = array.at[tuple(spot)].set(smallest)
    longest = extent.index(max(extent))
    spot[longest] = (spot[longest] + 1) % extent[longest]
    return array.at[tuple(spot)].set(high)


def levels(key, shape, cuts, least, high):
    level = 1.0
    for axis_at, blocks in cuts:
        heights = jax.random.uniform(jax.random.fold_in(jax.random.fold_in(key, 6), axis_at), (blocks,), jnp.float32, least / len(cuts), high / len(cuts))
        level = level * jnp.repeat(jnp.exp(heights), shape[axis_at] // blocks).reshape((-1,) + (1,) * (len(shape) - 1 - axis_at))
    return level


def gaussian(key, extent, width, bound, cuts=(), held_as=jnp.bfloat16):
    values = width * jax.random.normal(key, extent, jnp.float32)
    if cuts:
        values = values * levels(key, extent, cuts, -0.22, 0.18)
    return jnp.clip(values, -bound, bound).astype(held_as)


def setup_inputs(seed: int = 0) -> dict:
    splits = jax.random.split(jax.random.key(seed), 9)
    return {
        "pressure_prev": gaussian(splits[0], (NX, NY, NZ), 1.0, 6.0, ((0, 16), (1, 2)), jnp.float32),
        "pressure_now": gaussian(splits[1], (NX, NY, NZ), 1.0, 6.0, ((0, 16), (1, 2)), jnp.float32),
        "courant": jnp.clip(0.05 + 0.13000001 * jax.random.uniform(splits[2], (NX, NY, NZ), jnp.float32) ** levels(splits[2], (NX, NY, NZ), ((0, 16), (1, 2)), -0.2, 0.2), 0.05, 0.18),
        "perturbation": jnp.clip(jnp.exp(math.log(0.04) - 2.0794415 * jax.random.uniform(splits[3], (NX, NY, NZ), jnp.float32) ** levels(splits[3], (NX, NY, NZ), ((0, 16), (1, 2)), -0.2, 0.2)), 0.005, 0.04),
        "source_pos": jax.random.randint(splits[4], (3,), 0, min(NX, NY, NZ)).astype(jnp.int32),
        "wavelet": gaussian(splits[5], (NT,), 3.0, 8.0, (), jnp.float32),
        "rec_cells": plant(jax.random.randint(splits[6], (N_GX, N_GY, REC), 0, CX * CY * CZ), jax.random.fold_in(splits[6], 1), 0, (CX * CY * CZ) - 1).astype(jnp.int32),
        "observed": draw_observed(jax.random.fold_in(splits[8], 71), 0),
    }


COEF = (-205.0 / 72.0, 8.0 / 5.0, -1.0 / 5.0, 8.0 / 315.0, -1.0 / 560.0)


def laplace(padded):
    size_x = padded.shape[-3] - 8
    size_y = padded.shape[-2] - 8
    size_z = padded.shape[-1] - 8

    def part(off_x, off_y, off_z):
        return padded[..., off_x:off_x + size_x, off_y:off_y + size_y, off_z:off_z + size_z]

    total = (3.0 * COEF[0]) * part(4, 4, 4)
    for k in range(1, 5):
        total = total + COEF[k] * (part(4 + k, 4, 4) + part(4 - k, 4, 4) + part(4, 4 + k, 4)
                                   + part(4, 4 - k, 4) + part(4, 4, 4 + k) + part(4, 4, 4 - k))
    return total


def blur(field, axis):
    count = field.shape[axis] - 2
    return (0.25 * lax.slice_in_dim(field, 0, count, axis=axis)
            + 0.5 * lax.slice_in_dim(field, 1, 1 + count, axis=axis)
            + 0.25 * lax.slice_in_dim(field, 2, 2 + count, axis=axis))


def reference(pressure_prev, pressure_now, courant, perturbation, source_pos, wavelet, rec_cells, observed):
    p_old, p_cur = pressure_prev, pressure_now
    q_old = jnp.zeros_like(p_cur)
    q_cur = jnp.zeros_like(p_cur)
    loc_x = rec_cells // (CY * CZ)
    loc_y = (rec_cells // CZ) % CY
    loc_z = rec_cells % CZ
    glob_x = jnp.arange(N_GX, dtype=jnp.int32)[:, None, None] * CX + loc_x
    glob_y = jnp.arange(N_GY, dtype=jnp.int32)[None, :, None] * CY + loc_y
    synth_list = []
    born_list = []
    for step in range(NT):
        lap_p = laplace(jnp.pad(p_cur, 4))
        lap_q = laplace(jnp.pad(q_cur, 4))
        p_new = 2.0 * p_cur - p_old + courant * lap_p
        p_new = p_new.at[source_pos[0], source_pos[1], source_pos[2]].add(wavelet[step])
        q_new = 2.0 * q_cur - q_old + courant * lap_q + perturbation * lap_p
        synth_list.append(p_new[glob_x, glob_y, loc_z])
        born_list.append(q_new[glob_x, glob_y, loc_z])
        p_old, p_cur, q_old, q_cur = p_cur, p_new, q_cur, q_new
    synthetic = jnp.stack(synth_list, axis=2)
    born = jnp.stack(born_list, axis=2)
    residual = observed - synthetic
    numer = jnp.sum(residual * born)
    denom = jnp.sum(born * born)
    step_len = numer / (denom + 1e-6)
    predicted = residual - step_len * born
    smooth = jnp.pad(perturbation, 1)
    for axis in range(3):
        smooth = blur(smooth, axis)
    updated_model = courant + step_len * smooth
    return p_cur, q_cur, predicted, updated_model
```

```python
import functools

import jax
import jax.numpy as jnp
from jax import lax
from jax.experimental import pallas as pl
from jax.experimental.pallas import tpu as pltpu
from jax.sharding import PartitionSpec as P

COEF = (-205.0 / 72.0, 8.0 / 5.0, -1.0 / 5.0, 8.0 / 315.0, -1.0 / 560.0)
AXES = ("gx", "gy")
LANES = 128
F32 = jnp.float32

VMEM = pl.BlockSpec(memory_space=pltpu.VMEM)
SMEM = pl.BlockSpec(memory_space=pltpu.SMEM)


def struct(*shape):
    return jax.ShapeDtypeStruct(shape, F32)


def params():
    return pltpu.CompilerParams(vmem_limit_bytes=24 * 1024 * 1024)


def cost(flops, moved):
    return pl.CostEstimate(flops=flops, bytes_accessed=moved, transcendentals=0)


def near_pairs(count):
    return [(i, i ^ 1) for i in range(count)]


def far_pairs(count):
    pairs = []
    for i in range(1, count - 1, 2):
        pairs += [(i, i + 1), (i + 1, i)]
    return pairs


def diagonal(pairs_x, pairs_y, count_y):
    return [(a * count_y + b, c * count_y + d) for a, c in pairs_x for b, d in pairs_y]


def laplace(field, layer, row, rows, lane):
    centre = [field[layer, half, row : row + rows, :] for half in range(2)]
    totals = [(3.0 * COEF[0]) * value for value in centre]
    for k in range(1, 5):
        keep_up = lane < LANES - k
        keep_down = lane >= k
        up = [pltpu.roll(value, LANES - k, 1) for value in centre]
        down = [pltpu.roll(value, k, 1) for value in centre]
        depth = [
            jnp.where(keep_up, up[0], up[1]) + jnp.where(keep_down, down[0], 0.0),
            jnp.where(keep_up, up[1], 0.0) + jnp.where(keep_down, down[1], down[0]),
        ]
        for half in range(2):
            pair = (
                field[layer + k, half, row : row + rows, :]
                + field[layer - k, half, row : row + rows, :]
            )
            pair = pair + (
                field[layer, half, row + k : row + k + rows, :]
                + field[layer, half, row - k : row - k + rows, :]
            )
            totals[half] = totals[half] + COEF[k] * (pair + depth[half])
    return totals


def halves(value):
    return (value[..., :LANES], value[..., LANES:])


def put(target, layers, rows, value):
    for half, part in enumerate(halves(value)):
        target[layers, half, rows, :] = part


def place_wide(wide, scalars, own, near, far, strips, near_strips, corners, first):
    size_x, size_y, _ = own.shape
    par_x = scalars[0]
    par_y = scalars[1]
    inner = slice(16, 16 + size_y)
    put(wide, slice(8, 8 + size_x), inner, own[...])
    near_at = (size_x + 8) * (1 - par_x)
    far_at = (size_x + 8) * par_x
    put(wide, pl.ds(near_at, 8), inner, near[0:8])
    put(wide, pl.ds(far_at, 8), inner, far[0:8])
    for side in range(2):
        rows = slice(8, 16) if side == 0 else slice(16 + size_y, 24 + size_y)

        def fill(which, rows=rows):
            if which < len(strips):
                put(wide, slice(8, 8 + size_x), rows, strips[which][8 * first : 8 * first + 8])
                put(wide, pl.ds(near_at, 8), rows, near_strips[which][8 * first : 8 * first + 8])
                corner_at = 4 + (size_x + 4) * par_x
                put(wide, pl.ds(corner_at, 4), rows, corners[which][4 * first : 4 * first + 4])
            else:
                zero = jnp.zeros((size_x + 8, 8, 2 * LANES), F32)
                put(wide, slice(4, 12 + size_x), rows, zero)

        pl.when(par_y == 1 - side)(functools.partial(fill, 0))
        pl.when(par_y == side)(functools.partial(fill, 1))


def each_side(scalars, count, size_y, present, absent):
    par_y = scalars[1]
    for side in range(2):
        start = 0 if side == 0 else 8 + size_y
        for which in range(2):
            action = present if which < count else absent
            at = 1 - side if which == 0 else side
            pl.when(par_y == at)(functools.partial(action, start))


def send_strips(scalars, value, size_x, size_y):
    even = scalars[1] == 0
    low = value[:, 0:8, :]
    high = value[:, size_y - 8 : size_y, :]
    return [jnp.where(even, high, low), jnp.where(even, low, high)]


def step_pair_kernel(count, tangent, blank, *refs):
    refs = list(refs)
    scalars = refs.pop(0)
    if not tangent:
        wave = refs.pop(0)
    if not blank:
        own, near, far = refs[:3]
        refs = refs[3:]
        strips, refs = refs[:count], refs[count:]
        near_strips, refs = refs[:count], refs[count:]
        corners, refs = refs[:count], refs[count:]
        prev = refs.pop(0)
    speed = refs.pop(0)
    if tangent:
        drive1, drive2 = refs[:2]
        refs = refs[2:]
        partner_strips, refs = refs[:count], refs[count:]
    else:
        perturb = refs.pop(0)
    next1, next2 = refs[:2]
    refs = refs[2:]
    if not tangent:
        drive1, drive2 = refs[:2]
        refs = refs[2:]
    strip_out, refs = refs[:count], refs[count:]
    if tangent:
        corner_out, refs = refs[:count], refs[count:]
    size_x, size_y, _ = next2.shape
    par_x = scalars[0]
    inner = slice(8, 8 + size_y)

    def lanes(rows):
        return lax.broadcasted_iota(jnp.int32, (rows, LANES), 1)

    if not blank:
        wide = refs.pop(0)
        place_wide(
            wide, scalars, own, near, far, strips, near_strips, corners, 1 if tangent else 0
        )

        def advance(layer, start, rows):
            laps = laplace(wide, layer + 4, start + 8, rows, lanes(rows))
            span = slice(start, start + rows)
            for half in range(2):
                value = wide[layer + 4, half, start + 8 : start + 8 + rows, :]
                fresh = (
                    2.0 * value
                    - prev[layer, half, span, :]
                    + speed[layer, half, span, :] * laps[half]
                )
                if tangent:
                    fresh = fresh + drive1[layer, half, span, :]
                else:
                    drive1[layer, half, span, :] = perturb[layer, half, span, :] * laps[half]
                next1[layer, half, span, :] = fresh

        def main(layer, carry):
            advance(layer, 8, size_y)
            return carry

        lax.fori_loop(0, size_x + 8, main, 0)

        def present(start):
            def body(layer, carry):
                advance(layer, start, 8)
                return carry

            lax.fori_loop(4, 4 + size_x, body, 0)

        def absent(start):
            zero = jnp.zeros((size_x, 2, 8, LANES), F32)
            next1[4 : 4 + size_x, :, start : start + 8, :] = zero
            if not tangent:
                drive1[4 : 4 + size_x, :, start : start + 8, :] = zero

        each_side(scalars, count, size_y, present, absent)
    else:
        next1[...] = drive1[...]

    if not tangent:
        src_x, src_y, src_z = scalars[2], scalars[3], scalars[4]

        @pl.when((src_x >= -4) & (src_x < size_x + 4) & (src_y >= -8) & (src_y < size_y + 8))
        def _():
            half = lax.shift_right_logical(src_z, 7)
            hit = lax.broadcasted_iota(jnp.int32, (1, LANES), 1) == src_z - half * LANES
            row = next1[src_x + 4, half, pl.ds(src_y + 8, 1), :]
            next1[src_x + 4, half, pl.ds(src_y + 8, 1), :] = row + jnp.where(hit, wave[0], 0.0)

    def second(layer, carry):
        laps = laplace(next1, layer + 4, 8, size_y, lanes(size_y))
        for half in range(2):
            fresh = 2.0 * next1[layer + 4, half, inner, :]
            if not blank:
                fresh = fresh - wide[layer + 8, half, 16 : 16 + size_y, :]
            fresh = fresh + speed[layer + 4, half, inner, :] * laps[half]
            if tangent:
                fresh = fresh + drive2[layer, half]
            else:
                drive2[layer, half] = perturb[layer + 4, half, inner, :] * laps[half]
            next2[layer, :, half * LANES : (half + 1) * LANES] = fresh
        return carry

    lax.fori_loop(0, size_x, second, 0)

    if not tangent:

        @pl.when((src_x >= 0) & (src_x < size_x) & (src_y >= 0) & (src_y < size_y))
        def _():
            hit = lax.broadcasted_iota(jnp.int32, (1, 2 * LANES), 1) == src_z
            row = next2[src_x, pl.ds(src_y, 1), :]
            next2[src_x, pl.ds(src_y, 1), :] = row + jnp.where(hit, wave[1], 0.0)

    made = send_strips(scalars, next2[...], size_x, size_y)
    for which in range(count):
        if not tangent:
            strip_out[which][...] = made[which]
        else:
            strip_out[which][0:size_x] = partner_strips[which][...]
            strip_out[which][size_x : 2 * size_x] = made[which]
            facing = pl.ds((size_x - 4) * par_x, 4)
            corner_out[which][0:4] = partner_strips[which][facing]
            strip = strip_out[which][pl.ds(size_x + (size_x - 4) * par_x, 4)]
            corner_out[which][4:8] = strip


def wide_shape(shape):
    return pltpu.VMEM((shape[0] + 16, 2, shape[1] + 32, LANES), F32)


def ring_struct(shape):
    return struct(shape[0] + 8, 2, shape[1] + 16, LANES)


def pressure_steps(shape, count, scalars, wave, pieces, prev, speed, perturb):
    own, near, far, strips, near_strips, corners = pieces
    outs = [ring_struct(shape), struct(*shape), ring_struct(shape)]
    outs += [struct(shape[0], 2, shape[1], LANES)]
    outs += [struct(shape[0], 8, shape[2])] * count
    args = [own, near, far, *strips, *near_strips, *corners, prev, speed, perturb]
    out = pl.pallas_call(
        functools.partial(step_pair_kernel, count, False, False),
        out_shape=outs,
        in_specs=[SMEM, SMEM] + [VMEM] * len(args),
        out_specs=[VMEM] * len(outs),
        scratch_shapes=[wide_shape(shape)],
        compiler_params=params(),
        cost_estimate=cost(9_000_000, 4_000_000),
        name="pressure_steps",
    )(scalars, wave, *args)
    return out[0], out[1], out[2], out[3], list(out[4:])


def tangent_steps(shape, count, scalars, pieces, prev, speed, drive1, drive2, partner_strips):
    blank = pieces is None
    outs = [ring_struct(shape), struct(*shape)]
    outs += [struct(2 * shape[0], 8, shape[2])] * count
    outs += [struct(8, 8, shape[2])] * count
    args = []
    if not blank:
        own, near, far, strips, near_strips, corners = pieces
        args = [own, near, far, *strips, *near_strips, *corners, prev]
    args += [speed, drive1, drive2, *partner_strips]
    out = pl.pallas_call(
        functools.partial(step_pair_kernel, count, True, blank),
        out_shape=outs,
        in_specs=[SMEM] + [VMEM] * len(args),
        out_specs=[VMEM] * len(outs),
        scratch_shapes=[] if blank else [wide_shape(shape)],
        compiler_params=params(),
        cost_estimate=cost(9_000_000, 4_000_000),
        name="tangent_steps",
    )(scalars, *args)
    return out[0], out[1], list(out[2 : 2 + count]), list(out[2 + count :])


def pack_kernel(count, scalars, p_now, p_prev, speed, perturb, far, near, *outs):
    size_x, size_y, _ = p_now.shape
    par_x = scalars[0]
    far_face = pl.ds((size_x - 4) * par_x, 4)
    near_face = pl.ds((size_x - 4) * (1 - par_x), 4)
    for target, face in ((far, far_face), (near, near_face)):
        target[0:size_x] = p_now[...]
        for k, field in enumerate((p_prev, speed, perturb)):
            target[size_x + 4 * k : size_x + 4 * k + 4] = field[face]
    strips, corners = outs[:count], outs[count:]
    for k, field in enumerate((p_now, perturb, p_prev, speed)):
        made = send_strips(scalars, field[...], size_x, size_y)
        for which in range(count):
            strips[which][k * size_x : (k + 1) * size_x] = made[which]
    for which in range(count):
        for k in range(2):
            start = k * size_x + (size_x - 4) * par_x
            corners[which][4 * k : 4 * k + 4] = strips[which][pl.ds(start, 4)]


def pack(shape, count, scalars, p_now, p_prev, speed, perturb):
    outs = [struct(shape[0] + 12, shape[1], shape[2])] * 2
    outs += [struct(4 * shape[0], 8, shape[2])] * count
    outs += [struct(8, 8, shape[2])] * count
    out = pl.pallas_call(
        functools.partial(pack_kernel, count),
        out_shape=outs,
        in_specs=[SMEM] + [VMEM] * 4,
        out_specs=[VMEM] * len(outs),
        compiler_params=params(),
        cost_estimate=cost(10_000, 3_000_000),
        name="pack",
    )(scalars, p_now, p_prev, speed, perturb)
    return out[0], out[1], list(out[2 : 2 + count]), list(out[2 + count :])


def gather_ring_kernel(count, scalars, p_prev, speed, perturb, near, far, *refs):
    strips, refs = refs[:count], refs[count:]
    near_strips, refs = refs[:count], refs[count:]
    corners, targets = refs[:count], refs[count:]
    size_x, size_y, _ = p_prev.shape
    par_x, par_y = scalars[0], scalars[1]
    inner = slice(8, 8 + size_y)
    near_at = (size_x + 4) * (1 - par_x)
    far_at = (size_x + 4) * par_x
    for k, (own, target) in enumerate(zip((p_prev, speed, perturb), targets)):
        put(target, slice(4, 4 + size_x), inner, own[...])
        face = slice(size_x + 4 * k, size_x + 4 * k + 4)
        put(target, pl.ds(near_at, 4), inner, near[face])
        put(target, pl.ds(far_at, 4), inner, far[face])
        part = (2, 3, 1)[k]
        for side in range(2):
            rows = slice(0, 8) if side == 0 else slice(8 + size_y, 16 + size_y)

            def fill(which, k=k, rows=rows, target=target, part=part):
                if which < count:
                    base = part * size_x
                    put(target, slice(4, 4 + size_x), rows, strips[which][base : base + size_x])
                    if k == 2:
                        face = pl.ds(base + (size_x - 4) * par_x, 4)
                        put(target, pl.ds(near_at, 4), rows, near_strips[which][face])
                        put(target, pl.ds(far_at, 4), rows, corners[which][4:8])
                else:
                    zero = jnp.zeros((size_x + 8, 8, 2 * LANES), F32)
                    put(target, slice(0, 8 + size_x), rows, zero)

            pl.when(par_y == 1 - side)(functools.partial(fill, 0))
            pl.when(par_y == side)(functools.partial(fill, 1))


def gather_ring(shape, count, scalars, fields, near, far, strips, near_strips, corners):
    args = [*fields, near, far, *strips, *near_strips, *corners]
    return pl.pallas_call(
        functools.partial(gather_ring_kernel, count),
        out_shape=[ring_struct(shape)] * 3,
        in_specs=[SMEM] + [VMEM] * len(args),
        out_specs=[VMEM] * 3,
        compiler_params=params(),
        cost_estimate=cost(10_000, 4_000_000),
        name="gather_ring",
    )(scalars, *args)


def receive_kernel(cells, p1, p2, q1, q2, synth, born):
    size_x, size_y, size_z = p2.shape
    rows, count = size_x * size_y, cells.shape[1]
    flat = cells[...]
    shift = size_z.bit_length() - 1
    row_of = lax.shift_right_logical(flat, shift)
    depth_of = flat - lax.shift_left(row_of, shift)
    pick = lax.broadcasted_iota(jnp.int32, (rows, count), 0) == row_of
    pick = pick.astype(F32).astype(jnp.bfloat16)
    depth = lax.broadcasted_iota(jnp.int32, (LANES, count), 0)
    hits = [depth == depth_of, depth + LANES == depth_of]

    def at(parts):
        total = jnp.zeros((1, count), F32)
        for part, hit in zip(parts, hits):
            rest = part
            picked = None
            for _ in range(3):
                piece = rest.astype(jnp.bfloat16)
                rest = rest - piece.astype(F32)
                got = lax.dot_general(
                    piece, pick, (((0,), (0,)), ((), ())), preferred_element_type=F32
                )
                picked = got if picked is None else picked + got
            total = total + jnp.sum(jnp.where(hit, picked, 0.0), axis=0, keepdims=True)
        return total

    for one, two, target in ((p1, p2, synth), (q1, q2, born)):
        first = [
            one[4 : 4 + size_x, half, 8 : 8 + size_y, :].reshape(rows, LANES) for half in range(2)
        ]
        target[0:1, :] = at(first)
        second = [part.reshape(rows, LANES) for part in halves(two[...])]
        target[1:2, :] = at(second)


def receive(cells, p1, p2, q1, q2):
    count = cells.shape[1]
    return pl.pallas_call(
        receive_kernel,
        out_shape=[struct(2, count)] * 2,
        in_specs=[VMEM] * 5,
        out_specs=[VMEM] * 2,
        compiler_params=params(),
        cost_estimate=cost(20_000_000, 2_500_000),
        name="receive",
    )(cells, p1, p2, q1, q2)


def smooth_kernel(perturb, smooth):
    size_x, size_y, _ = smooth.shape
    lane = lax.broadcasted_iota(jnp.int32, (size_y, LANES), 1)

    def layer_step(layer, carry):
        parts = []
        for half in range(2):

            def along_x(start, half=half):
                span = slice(start, start + size_y)
                return (
                    0.25 * perturb[layer + 3, half, span, :]
                    + 0.5 * perturb[layer + 4, half, span, :]
                    + 0.25 * perturb[layer + 5, half, span, :]
                )

            parts.append(0.25 * along_x(7) + 0.5 * along_x(8) + 0.25 * along_x(9))
        up = [pltpu.roll(value, LANES - 1, 1) for value in parts]
        down = [pltpu.roll(value, 1, 1) for value in parts]
        keep_up, keep_down = lane < LANES - 1, lane >= 1
        above = [jnp.where(keep_up, up[0], up[1]), jnp.where(keep_up, up[1], 0.0)]
        below = [jnp.where(keep_down, down[0], 0.0), jnp.where(keep_down, down[1], down[0])]
        for half in range(2):
            value = 0.25 * below[half] + 0.5 * parts[half] + 0.25 * above[half]
            smooth[layer, :, half * LANES : (half + 1) * LANES] = value
        return carry

    lax.fori_loop(0, size_x, layer_step, 0)


def smoothed(shape, perturb):
    return pl.pallas_call(
        smooth_kernel,
        out_shape=struct(*shape),
        in_specs=[VMEM],
        out_specs=VMEM,
        compiler_params=params(),
        cost_estimate=cost(1_000_000, 1_200_000),
        name="smooth",
    )(perturb)


def on_device(
    pressure_prev, pressure_now, courant, perturbation, source_pos, wavelet, rec_cells, observed
):
    shape = pressure_now.shape
    size_x, size_y, size_z = shape
    count_x, count_y = lax.axis_size("gx"), lax.axis_size("gy")
    place_x, place_y = lax.axis_index("gx"), lax.axis_index("gy")
    steps = wavelet.shape[0]
    scalars = jnp.stack(
        [
            place_x % 2,
            place_y % 2,
            source_pos[0] - place_x * size_x,
            source_pos[1] - place_y * size_y,
            source_pos[2],
        ]
    ).astype(jnp.int32)
    near_x, far_x = near_pairs(count_x), far_pairs(count_x)
    pairs_y = [near_pairs(count_y)]
    if count_y > 2:
        pairs_y.append(far_pairs(count_y))
    count = len(pairs_y)
    far_diagonal = [diagonal(far_x, pairs, count_y) for pairs in pairs_y]

    def swap_near(value):
        return lax.ppermute(value, "gx", near_x)

    def swap_far(value):
        return lax.ppermute(value, "gx", far_x)

    def swap_strips(strips, corners):
        got = [lax.ppermute(value, "gy", pairs) for value, pairs in zip(strips, pairs_y)]
        got_corners = [
            lax.ppermute(value, AXES, pairs) for value, pairs in zip(corners, far_diagonal)
        ]
        return got, [swap_near(value) for value in got], got_corners

    far_send, near_send, strips, corners = pack(
        shape, count, scalars, pressure_now, pressure_prev, courant, perturbation
    )
    far, near = swap_far(far_send), swap_near(near_send)
    strips, near_strips, corners = swap_strips(strips, corners)
    p_prev, speed, perturb = gather_ring(
        shape,
        count,
        scalars,
        (pressure_prev, courant, perturbation),
        near,
        far,
        strips,
        near_strips,
        corners,
    )
    smooth = smoothed(shape, perturb)
    cells = rec_cells.reshape(1, -1)
    p_cur, q_cur, q_prev = pressure_now, None, None
    p_far, p_near = far, near
    q_far = q_near = None
    synth_list, born_list = [], []
    for step in range(0, steps, 2):
        wave = lax.slice_in_dim(wavelet, step, step + 2)
        around = (strips, near_strips, corners)
        p_pieces = (p_cur, p_near, p_far) + around
        q_pieces = None if q_cur is None else (q_cur, q_near, q_far) + around
        p_prev, p_cur, drive1, drive2, p_strips = pressure_steps(
            shape, count, scalars, wave, p_pieces, p_prev, speed, perturb
        )
        last = step + 2 >= steps
        if not last:
            p_far, p_near = swap_far(p_cur), swap_near(p_cur)
        q_prev, q_cur, strips, corners = tangent_steps(
            shape, count, scalars, q_pieces, q_prev, speed, drive1, drive2, p_strips
        )
        if not last:
            strips, near_strips, corners = swap_strips(strips, corners)
            q_far, q_near = swap_far(q_cur), swap_near(q_cur)
        synth, born = receive(cells, p_prev, p_cur, q_prev, q_cur)
        synth_list.append(synth)
        born_list.append(born)
    synthetic = jnp.concatenate(synth_list, axis=0)
    born = jnp.concatenate(born_list, axis=0)
    residual = observed.reshape(born.shape) - synthetic
    sums = jnp.stack([jnp.sum(residual * born), jnp.sum(born * born)])
    total = count_x * count_y
    spread = jnp.broadcast_to(sums.reshape(1, 1, 2), (total, 1, 2))
    sums = jnp.sum(lax.all_to_all(spread, AXES, 0, 0), axis=(0, 1))
    step_len = sums[0] / (sums[1] + 1e-6)
    predicted = (residual - step_len * born).reshape(observed.shape)
    updated_model = courant + step_len * smooth
    return (p_cur, q_cur, predicted, updated_model)


def solution(mesh):
    field = P("gx", "gy", None)
    traces = P("gx", "gy", None, None)
    return jax.shard_map(
        on_device,
        mesh=mesh,
        in_specs=(field, field, field, field, P(), P(), field, traces),
        out_specs=(field, field, traces, field),
        check_vma=False,
    )
```

```python
import functools

import jax
import jax.numpy as jnp
from jax import lax
from jax.experimental import pallas as pl
from jax.experimental.pallas import tpu as pltpu
from jax.sharding import PartitionSpec as P

COEF = (-205.0 / 72.0, 8.0 / 5.0, -1.0 / 5.0, 8.0 / 315.0, -1.0 / 560.0)
AXES = ("gx", "gy")
LANES = 128
F32 = jnp.float32

VMEM = pl.BlockSpec(memory_space=pltpu.VMEM)
SMEM = pl.BlockSpec(memory_space=pltpu.SMEM)


def struct(*shape):
    return jax.ShapeDtypeStruct(shape, F32)


def params():
    return pltpu.CompilerParams(vmem_limit_bytes=24 * 1024 * 1024)


def cost(flops, moved):
    return pl.CostEstimate(flops=flops, bytes_accessed=moved, transcendentals=0)


def near_pairs(count):
    return [(i, i ^ 1) for i in range(count)]


def far_pairs(count):
    pairs = []
    for i in range(1, count - 1, 2):
        pairs += [(i, i + 1), (i + 1, i)]
    return pairs


def diagonal(pairs_x, pairs_y, count_y):
    return [(a * count_y + b, c * count_y + d) for a, c in pairs_x for b, d in pairs_y]


def parity():
    return lax.rem(lax.axis_index("gx"), 2), lax.rem(lax.axis_index("gy"), 2)


def laplace(field, layer, row, rows, lane):
    centre = [field[layer, half, row : row + rows, :] for half in range(2)]
    totals = [(3.0 * COEF[0]) * value for value in centre]
    for k in range(1, 5):
        keep_up = lane < LANES - k
        keep_down = lane >= k
        up = [pltpu.roll(value, LANES - k, 1) for value in centre]
        down = [pltpu.roll(value, k, 1) for value in centre]
        depth = [
            jnp.where(keep_up, up[0], up[1]) + jnp.where(keep_down, down[0], 0.0),
            jnp.where(keep_up, up[1], 0.0) + jnp.where(keep_down, down[1], down[0]),
        ]
        for half in range(2):
            pair = (
                field[layer + k, half, row : row + rows, :]
                + field[layer - k, half, row : row + rows, :]
            )
            pair = pair + (
                field[layer, half, row + k : row + k + rows, :]
                + field[layer, half, row - k : row - k + rows, :]
            )
            totals[half] = totals[half] + COEF[k] * (pair + depth[half])
    return totals


def halves(value):
    return (value[..., :LANES], value[..., LANES:])


def put(target, layers, rows, value):
    for half, part in enumerate(halves(value)):
        target[layers, half, rows, :] = part


def place_wide(wide, scalars, own, near, far, strips, near_strips, corners, first):
    size_x, size_y, _ = own.shape
    par_x = scalars[0]
    par_y = scalars[1]
    inner = slice(16, 16 + size_y)
    put(wide, slice(8, 8 + size_x), inner, own[...])
    near_at = (size_x + 8) * (1 - par_x)
    far_at = (size_x + 8) * par_x
    put(wide, pl.ds(near_at, 8), inner, near[0:8])
    put(wide, pl.ds(far_at, 8), inner, far[0:8])
    for side in range(2):
        rows = slice(8, 16) if side == 0 else slice(16 + size_y, 24 + size_y)

        def fill(which, rows=rows):
            if which < len(strips):
                put(wide, slice(8, 8 + size_x), rows, strips[which][8 * first : 8 * first + 8])
                put(wide, pl.ds(near_at, 8), rows, near_strips[which][8 * first : 8 * first + 8])
                corner_at = 4 + (size_x + 4) * par_x
                put(wide, pl.ds(corner_at, 4), rows, corners[which][4 * first : 4 * first + 4])
            else:
                zero = jnp.zeros((size_x + 8, 8, 2 * LANES), F32)
                put(wide, slice(4, 12 + size_x), rows, zero)

        pl.when(par_y == 1 - side)(functools.partial(fill, 0))
        pl.when(par_y == side)(functools.partial(fill, 1))


def each_side(scalars, count, size_y, present, absent):
    par_y = scalars[1]
    for side in range(2):
        start = 0 if side == 0 else 8 + size_y
        for which in range(2):
            action = present if which < count else absent
            at = 1 - side if which == 0 else side
            pl.when(par_y == at)(functools.partial(action, start))


def send_strips(scalars, value, size_x, size_y):
    even = scalars[1] == 0
    low = value[:, 0:8, :]
    high = value[:, size_y - 8 : size_y, :]
    return [jnp.where(even, high, low), jnp.where(even, low, high)]


def step_pair_kernel(count, tangent, blank, at, *refs):
    refs = list(refs)
    scalars = parity()
    if not tangent:
        source, wave = refs[:2]
        refs = refs[2:]
    if not blank:
        own, near, far = refs[:3]
        refs = refs[3:]
        strips, refs = refs[:count], refs[count:]
        near_strips, refs = refs[:count], refs[count:]
        corners, refs = refs[:count], refs[count:]
        prev = refs.pop(0)
    speed = refs.pop(0)
    if tangent:
        drive1, drive2 = refs[:2]
        refs = refs[2:]
        partner_strips, refs = refs[:count], refs[count:]
    else:
        perturb = refs.pop(0)
    next1, next2 = refs[:2]
    refs = refs[2:]
    if not tangent:
        drive1, drive2 = refs[:2]
        refs = refs[2:]
    strip_out, refs = refs[:count], refs[count:]
    if tangent:
        corner_out, refs = refs[:count], refs[count:]
    size_x, size_y, _ = next2.shape
    par_x = scalars[0]
    inner = slice(8, 8 + size_y)

    def lanes(rows):
        return lax.broadcasted_iota(jnp.int32, (rows, LANES), 1)

    if not blank:
        wide = refs.pop(0)
        place_wide(
            wide, scalars, own, near, far, strips, near_strips, corners, 1 if tangent else 0
        )

        def advance(layer, start, rows):
            laps = laplace(wide, layer + 4, start + 8, rows, lanes(rows))
            span = slice(start, start + rows)
            for half in range(2):
                value = wide[layer + 4, half, start + 8 : start + 8 + rows, :]
                fresh = (
                    2.0 * value
                    - prev[layer, half, span, :]
                    + speed[layer, half, span, :] * laps[half]
                )
                if tangent:
                    fresh = fresh + drive1[layer, half, span, :]
                else:
                    drive1[layer, half, span, :] = perturb[layer, half, span, :] * laps[half]
                next1[layer, half, span, :] = fresh

        for layer in range(size_x + 8):
            advance(layer, 8, size_y)

        def present(start):
            for layer in range(4, 4 + size_x):
                advance(layer, start, 8)

        def absent(start):
            zero = jnp.zeros((size_x, 2, 8, LANES), F32)
            next1[4 : 4 + size_x, :, start : start + 8, :] = zero
            if not tangent:
                drive1[4 : 4 + size_x, :, start : start + 8, :] = zero

        each_side(scalars, count, size_y, present, absent)
    else:
        next1[...] = drive1[...]

    if not tangent:
        src_x = source[0] - lax.axis_index("gx") * size_x
        src_y = source[1] - lax.axis_index("gy") * size_y
        src_z = source[2]

        @pl.when((src_x >= -4) & (src_x < size_x + 4) & (src_y >= -8) & (src_y < size_y + 8))
        def _():
            half = lax.shift_right_logical(src_z, 7)
            hit = lax.broadcasted_iota(jnp.int32, (1, LANES), 1) == src_z - half * LANES
            row = next1[src_x + 4, half, pl.ds(src_y + 8, 1), :]
            next1[src_x + 4, half, pl.ds(src_y + 8, 1), :] = row + jnp.where(hit, wave[at], 0.0)

    for layer in range(size_x):
        laps = laplace(next1, layer + 4, 8, size_y, lanes(size_y))
        for half in range(2):
            fresh = 2.0 * next1[layer + 4, half, inner, :]
            if not blank:
                fresh = fresh - wide[layer + 8, half, 16 : 16 + size_y, :]
            fresh = fresh + speed[layer + 4, half, inner, :] * laps[half]
            if tangent:
                fresh = fresh + drive2[layer, half]
            else:
                drive2[layer, half] = perturb[layer + 4, half, inner, :] * laps[half]
            next2[layer, :, half * LANES : (half + 1) * LANES] = fresh

    if not tangent:

        @pl.when((src_x >= 0) & (src_x < size_x) & (src_y >= 0) & (src_y < size_y))
        def _():
            hit = lax.broadcasted_iota(jnp.int32, (1, 2 * LANES), 1) == src_z
            row = next2[src_x, pl.ds(src_y, 1), :]
            next2[src_x, pl.ds(src_y, 1), :] = row + jnp.where(hit, wave[at + 1], 0.0)

    made = send_strips(scalars, next2[...], size_x, size_y)
    for which in range(count):
        if not tangent:
            strip_out[which][...] = made[which]
        else:
            strip_out[which][0:size_x] = partner_strips[which][...]
            strip_out[which][size_x : 2 * size_x] = made[which]
            facing = pl.ds((size_x - 4) * par_x, 4)
            corner_out[which][0:4] = partner_strips[which][facing]
            strip = strip_out[which][pl.ds(size_x + (size_x - 4) * par_x, 4)]
            corner_out[which][4:8] = strip


def wide_shape(shape):
    return pltpu.VMEM((shape[0] + 16, 2, shape[1] + 32, LANES), F32)


def ring_struct(shape):
    return struct(shape[0] + 8, 2, shape[1] + 16, LANES)


def pressure_steps(shape, count, at, source, wave, pieces, prev, speed, perturb):
    own, near, far, strips, near_strips, corners = pieces
    outs = [ring_struct(shape), struct(*shape), ring_struct(shape)]
    outs += [struct(shape[0], 2, shape[1], LANES)]
    outs += [struct(shape[0], 8, shape[2])] * count
    args = [own, near, far, *strips, *near_strips, *corners, prev, speed, perturb]
    out = pl.pallas_call(
        functools.partial(step_pair_kernel, count, False, False, at),
        out_shape=outs,
        in_specs=[SMEM, SMEM] + [VMEM] * len(args),
        out_specs=[VMEM] * len(outs),
        scratch_shapes=[wide_shape(shape)],
        compiler_params=params(),
        cost_estimate=cost(9_000_000, 4_000_000),
        name="pressure_steps",
    )(source, wave, *args)
    return out[0], out[1], out[2], out[3], list(out[4:])


def tangent_steps(shape, count, pieces, prev, speed, drive1, drive2, partner_strips):
    blank = pieces is None
    outs = [ring_struct(shape), struct(*shape)]
    outs += [struct(2 * shape[0], 8, shape[2])] * count
    outs += [struct(8, 8, shape[2])] * count
    args = []
    if not blank:
        own, near, far, strips, near_strips, corners = pieces
        args = [own, near, far, *strips, *near_strips, *corners, prev]
    args += [speed, drive1, drive2, *partner_strips]
    out = pl.pallas_call(
        functools.partial(step_pair_kernel, count, True, blank, 0),
        out_shape=outs,
        in_specs=[VMEM] * len(args),
        out_specs=[VMEM] * len(outs),
        scratch_shapes=[] if blank else [wide_shape(shape)],
        compiler_params=params(),
        cost_estimate=cost(9_000_000, 4_000_000),
        name="tangent_steps",
    )(*args)
    return out[0], out[1], list(out[2 : 2 + count]), list(out[2 + count :])


def pack_kernel(count, p_now, p_prev, speed, perturb, far, near, *rest):
    size_x, size_y, _ = p_now.shape
    strips, corners, sems = rest[:count], rest[count : 2 * count], rest[2 * count]
    par_x, par_y = parity()
    far_face = pl.ds((size_x - 4) * par_x, 4)
    near_face = pl.ds((size_x - 4) * (1 - par_x), 4)
    moves = []
    for target, face in ((far, far_face), (near, near_face)):
        moves.append((p_now, target.at[0:size_x]))
        for k, field in enumerate((p_prev, speed, perturb)):
            start = size_x + 4 * k
            moves.append((field.at[face], target.at[start : start + 4]))
    for which in range(count):
        high = 1 - par_y if which == 0 else par_y
        rows = pl.ds(pl.multiple_of(high * (size_y - 8), 8), 8)
        for k, field in enumerate((p_now, perturb, p_prev, speed)):
            moves.append((field.at[:, rows], strips[which].at[k * size_x : (k + 1) * size_x]))
            if k < 2:
                moves.append((field.at[far_face, rows], corners[which].at[4 * k : 4 * k + 4]))
    copies = [
        pltpu.make_async_copy(source, target, sems.at[k]) for k, (source, target) in enumerate(moves)
    ]
    for copy in copies:
        copy.start()
    for copy in copies:
        copy.wait()


def pack(shape, count, p_now, p_prev, speed, perturb):
    outs = [struct(shape[0] + 12, shape[1], shape[2])] * 2
    outs += [struct(4 * shape[0], 8, shape[2])] * count
    outs += [struct(8, 8, shape[2])] * count
    out = pl.pallas_call(
        functools.partial(pack_kernel, count),
        out_shape=outs,
        in_specs=[pl.BlockSpec(memory_space=pl.ANY)] * 4,
        out_specs=[VMEM] * len(outs),
        scratch_shapes=[pltpu.SemaphoreType.DMA((8 + 6 * count,))],
        compiler_params=params(),
        cost_estimate=cost(10_000, 3_000_000),
        name="pack",
    )(p_now, p_prev, speed, perturb)
    return out[0], out[1], list(out[2 : 2 + count]), list(out[2 + count :])


def gather_ring_kernel(count, p_prev, speed, perturb, near, far, *refs):
    strips, refs = refs[:count], refs[count:]
    near_strips, refs = refs[:count], refs[count:]
    corners, targets = refs[:count], refs[count:]
    size_x, size_y, _ = p_prev.shape
    par_x, par_y = parity()
    inner = slice(8, 8 + size_y)
    near_at = (size_x + 4) * (1 - par_x)
    far_at = (size_x + 4) * par_x
    for k, (own, target) in enumerate(zip((p_prev, speed, perturb), targets)):
        put(target, slice(4, 4 + size_x), inner, own[...])
        face = slice(size_x + 4 * k, size_x + 4 * k + 4)
        put(target, pl.ds(near_at, 4), inner, near[face])
        put(target, pl.ds(far_at, 4), inner, far[face])
        part = (2, 3, 1)[k]
        for side in range(2):
            rows = slice(0, 8) if side == 0 else slice(8 + size_y, 16 + size_y)

            def fill(which, k=k, rows=rows, target=target, part=part):
                if which < count:
                    base = part * size_x
                    put(target, slice(4, 4 + size_x), rows, strips[which][base : base + size_x])
                    if k == 2:
                        face = pl.ds(base + (size_x - 4) * par_x, 4)
                        put(target, pl.ds(near_at, 4), rows, near_strips[which][face])
                        put(target, pl.ds(far_at, 4), rows, corners[which][4:8])
                else:
                    zero = jnp.zeros((size_x + 8, 8, 2 * LANES), F32)
                    put(target, slice(0, 8 + size_x), rows, zero)

            pl.when(par_y == 1 - side)(functools.partial(fill, 0))
            pl.when(par_y == side)(functools.partial(fill, 1))


def gather_ring(shape, count, fields, near, far, strips, near_strips, corners):
    args = [*fields, near, far, *strips, *near_strips, *corners]
    return pl.pallas_call(
        functools.partial(gather_ring_kernel, count),
        out_shape=[ring_struct(shape)] * 3,
        in_specs=[VMEM] * len(args),
        out_specs=[VMEM] * 3,
        compiler_params=params(),
        cost_estimate=cost(10_000, 4_000_000),
        name="gather_ring",
    )(*args)


def receive_kernel(rounds, cells, p1, p2, q1, q2, *refs):
    size_x, size_y, size_z = p2.shape
    if rounds:
        earlier, observed = refs[: 2 * rounds], refs[2 * rounds]
        synth, born, spread = refs[2 * rounds + 1 :]
    else:
        synth, born = refs
    steps = synth.shape[0]
    rows, count = size_x * size_y, cells.shape[1]
    flat = cells[...]
    shift = size_z.bit_length() - 1
    row_of = lax.shift_right_logical(flat, shift)
    depth_of = flat - lax.shift_left(row_of, shift)
    pick = lax.broadcasted_iota(jnp.int32, (rows, count), 0) == row_of
    pick = pick.astype(F32).astype(jnp.bfloat16)
    depth = lax.broadcasted_iota(jnp.int32, (LANES, count), 0)
    hits = [depth == depth_of, depth + LANES == depth_of]

    def at(parts):
        total = jnp.zeros((1, count), F32)
        for part, hit in zip(parts, hits):
            rest = part
            picked = None
            for _ in range(3):
                piece = rest.astype(jnp.bfloat16)
                rest = rest - piece.astype(F32)
                got = lax.dot_general(
                    piece, pick, (((0,), (0,)), ((), ())), preferred_element_type=F32
                )
                picked = got if picked is None else picked + got
            total = total + jnp.sum(jnp.where(hit, picked, 0.0), axis=0, keepdims=True)
        return total

    for one, two, target in ((p1, p2, synth), (q1, q2, born)):
        first = [
            one[4 : 4 + size_x, half, 8 : 8 + size_y, :].reshape(rows, LANES) for half in range(2)
        ]
        target[steps - 2 : steps - 1, :] = at(first)
        second = [part.reshape(rows, LANES) for part in halves(two[...])]
        target[steps - 1 : steps, :] = at(second)


    if rounds:
        for k in range(rounds):
            synth[2 * k : 2 * k + 2, :] = earlier[2 * k][...]
            born[2 * k : 2 * k + 2, :] = earlier[2 * k + 1][...]
        residual = observed[...] - synth[...]
        tangent = born[...]
        synth[...] = residual
        numer, denom = jnp.sum(residual * tangent), jnp.sum(tangent * tangent)
        lane = lax.broadcasted_iota(jnp.int32, spread.shape, 2)
        spread[...] = jnp.where(lane == 0, numer, jnp.where(lane == 1, denom, 0.0))


def receive(cells, p1, p2, q1, q2, earlier=(), observed=None, total=0):
    count = cells.shape[1]
    rounds = len(earlier) // 2
    outs = [struct(2 * rounds + 2, count)] * 2
    args = [cells, p1, p2, q1, q2]
    if rounds:
        outs.append(struct(total, 1, LANES))
        args += [*earlier, observed]
    return pl.pallas_call(
        functools.partial(receive_kernel, rounds),
        out_shape=outs,
        in_specs=[VMEM] * len(args),
        out_specs=[VMEM] * len(outs),
        compiler_params=params(),
        cost_estimate=cost(20_000_000, 2_500_000),
        name="receive",
    )(*args)


def finish_kernel(sums, residual, born, speed, smooth, predicted, model, traces, field, sems):
    lane = lax.broadcasted_iota(jnp.int32, sums.shape, 2)
    values = sums[...]
    numer = jnp.sum(jnp.where(lane == 0, values, 0.0))
    denom = jnp.sum(jnp.where(lane == 1, values, 0.0))
    length = jnp.full((1, LANES), numer) / (jnp.full((1, LANES), denom) + 1e-6)
    traces[...] = residual[...] - length * born[...]
    first = pltpu.make_async_copy(traces, predicted, sems.at[0])
    first.start()
    both = jnp.concatenate([length, length], axis=1)
    field[...] = speed[...] + both[None] * smooth[...]
    second = pltpu.make_async_copy(field, model, sems.at[1])
    second.start()
    first.wait()
    second.wait()


def finish(sums, residual, born, speed, smooth):
    outs = [struct(*born.shape), struct(*speed.shape)]
    return pl.pallas_call(
        finish_kernel,
        out_shape=outs,
        in_specs=[VMEM] * 5,
        out_specs=[pl.BlockSpec(memory_space=pl.ANY)] * 2,
        scratch_shapes=[
            pltpu.VMEM(born.shape, F32),
            pltpu.VMEM(speed.shape, F32),
            pltpu.SemaphoreType.DMA((2,)),
        ],
        compiler_params=params(),
        cost_estimate=cost(200_000, 800_000),
        name="finish",
    )(sums, residual, born, speed, smooth)


def smooth_kernel(perturb, smooth):
    size_x, size_y, _ = smooth.shape
    lane = lax.broadcasted_iota(jnp.int32, (size_y, LANES), 1)

    def layer_step(layer, carry):
        parts = []
        for half in range(2):

            def along_x(start, half=half):
                span = slice(start, start + size_y)
                return (
                    0.25 * perturb[layer + 3, half, span, :]
                    + 0.5 * perturb[layer + 4, half, span, :]
                    + 0.25 * perturb[layer + 5, half, span, :]
                )

            parts.append(0.25 * along_x(7) + 0.5 * along_x(8) + 0.25 * along_x(9))
        up = [pltpu.roll(value, LANES - 1, 1) for value in parts]
        down = [pltpu.roll(value, 1, 1) for value in parts]
        keep_up, keep_down = lane < LANES - 1, lane >= 1
        above = [jnp.where(keep_up, up[0], up[1]), jnp.where(keep_up, up[1], 0.0)]
        below = [jnp.where(keep_down, down[0], 0.0), jnp.where(keep_down, down[1], down[0])]
        for half in range(2):
            value = 0.25 * below[half] + 0.5 * parts[half] + 0.25 * above[half]
            smooth[layer, :, half * LANES : (half + 1) * LANES] = value
        return carry

    lax.fori_loop(0, size_x, layer_step, 0)


def smoothed(shape, perturb):
    return pl.pallas_call(
        smooth_kernel,
        out_shape=struct(*shape),
        in_specs=[VMEM],
        out_specs=VMEM,
        compiler_params=params(),
        cost_estimate=cost(1_000_000, 1_200_000),
        name="smooth",
    )(perturb)


def on_device(
    pressure_prev, pressure_now, courant, perturbation, source_pos, wavelet, rec_cells, observed
):
    shape = pressure_now.shape
    size_x, size_y, size_z = shape
    count_x, count_y = lax.axis_size("gx"), lax.axis_size("gy")
    steps = wavelet.shape[0]
    near_x, far_x = near_pairs(count_x), far_pairs(count_x)
    pairs_y = [near_pairs(count_y)]
    if count_y > 2:
        pairs_y.append(far_pairs(count_y))
    count = len(pairs_y)
    far_diagonal = [diagonal(far_x, pairs, count_y) for pairs in pairs_y]

    def swap_near(value):
        return lax.ppermute(value, "gx", near_x)

    def swap_far(value):
        return lax.ppermute(value, "gx", far_x)

    def swap_strips(strips, corners):
        got = [lax.ppermute(value, "gy", pairs) for value, pairs in zip(strips, pairs_y)]
        got_corners = [
            lax.ppermute(value, AXES, pairs) for value, pairs in zip(corners, far_diagonal)
        ]
        return got, [swap_near(value) for value in got], got_corners

    far_send, near_send, strips, corners = pack(
        shape, count, pressure_now, pressure_prev, courant, perturbation
    )
    far, near = swap_far(far_send), swap_near(near_send)
    strips, near_strips, corners = swap_strips(strips, corners)
    p_prev, speed, perturb = gather_ring(
        shape,
        count,
        (pressure_prev, courant, perturbation),
        near,
        far,
        strips,
        near_strips,
        corners,
    )
    smooth = smoothed(shape, perturb)
    cells = rec_cells.reshape(1, -1)
    p_cur, q_cur, q_prev = pressure_now, None, None
    p_far, p_near = far, near
    q_far = q_near = None
    earlier = []
    for step in range(0, steps, 2):
        around = (strips, near_strips, corners)
        p_pieces = (p_cur, p_near, p_far) + around
        q_pieces = None if q_cur is None else (q_cur, q_near, q_far) + around
        p_prev, p_cur, drive1, drive2, p_strips = pressure_steps(
            shape, count, step, source_pos, wavelet, p_pieces, p_prev, speed, perturb
        )
        last = step + 2 >= steps
        if not last:
            p_far, p_near = swap_far(p_cur), swap_near(p_cur)
        q_prev, q_cur, strips, corners = tangent_steps(
            shape, count, q_pieces, q_prev, speed, drive1, drive2, p_strips
        )
        if not last:
            strips, near_strips, corners = swap_strips(strips, corners)
            q_far, q_near = swap_far(q_cur), swap_near(q_cur)
        if not last:
            earlier += receive(cells, p_prev, p_cur, q_prev, q_cur)
    total = count_x * count_y
    observed_traces = observed.reshape(steps, -1)
    residual, born, spread = receive(
        cells, p_prev, p_cur, q_prev, q_cur, earlier, observed_traces, total
    )
    sums = lax.all_to_all(spread, AXES, 0, 0)
    predicted, updated_model = finish(sums, residual, born, courant, smooth)
    predicted = predicted.reshape(observed.shape)
    return (p_cur, q_cur, predicted, updated_model)


def solution(mesh):
    field = P("gx", "gy", None)
    traces = P("gx", "gy", None, None)
    return jax.shard_map(
        on_device,
        mesh=mesh,
        in_specs=(field, field, field, field, P(), P(), field, traces),
        out_specs=(field, field, traces, field),
        check_vma=False,
    )
```

```python
import functools

import jax
import jax.numpy as jnp
from jax import lax
from jax.experimental import pallas as pl
from jax.experimental.pallas import tpu as pltpu
from jax.sharding import PartitionSpec as P

COEF = (-205.0 / 72.0, 8.0 / 5.0, -1.0 / 5.0, 8.0 / 315.0, -1.0 / 560.0)
AXES = ("gx", "gy")
LANES = 128
F32 = jnp.float32

VMEM = pl.BlockSpec(memory_space=pltpu.VMEM)


def struct(*shape):
    return jax.ShapeDtypeStruct(shape, F32)


def params():
    return pltpu.CompilerParams(vmem_limit_bytes=24 * 1024 * 1024)


def cost(flops, moved):
    return pl.CostEstimate(flops=flops, bytes_accessed=moved, transcendentals=0)


def near_pairs(count):
    return [(i, i ^ 1) for i in range(count)]


def far_pairs(count):
    pairs = []
    for i in range(1, count - 1, 2):
        pairs += [(i, i + 1), (i + 1, i)]
    return pairs


def diagonal(pairs_x, pairs_y, count_y):
    return [(a * count_y + b, c * count_y + d) for a, c in pairs_x for b, d in pairs_y]


def parity():
    return lax.rem(lax.axis_index("gx"), 2), lax.rem(lax.axis_index("gy"), 2)


def laplace(field, layer, row, rows, lane):
    centre = [field[layer, half, row : row + rows, :] for half in range(2)]
    totals = [(3.0 * COEF[0]) * value for value in centre]
    for k in range(1, 5):
        keep_up = lane < LANES - k
        keep_down = lane >= k
        up = [pltpu.roll(value, LANES - k, 1) for value in centre]
        down = [pltpu.roll(value, k, 1) for value in centre]
        depth = [
            jnp.where(keep_up, up[0], up[1]) + jnp.where(keep_down, down[0], 0.0),
            jnp.where(keep_up, up[1], 0.0) + jnp.where(keep_down, down[1], down[0]),
        ]
        for half in range(2):
            pair = (
                field[layer + k, half, row : row + rows, :]
                + field[layer - k, half, row : row + rows, :]
            )
            pair = pair + (
                field[layer, half, row + k : row + k + rows, :]
                + field[layer, half, row - k : row - k + rows, :]
            )
            totals[half] = totals[half] + COEF[k] * (pair + depth[half])
    return totals


def halves(value):
    return (value[..., :LANES], value[..., LANES:])


def put(target, layers, rows, value):
    for half, part in enumerate(halves(value)):
        target[layers, half, rows, :] = part


def place_wide(wide, scalars, own, near, far, strips, near_strips, corners, first):
    size_x, size_y, _ = own.shape
    par_x = scalars[0]
    par_y = scalars[1]
    inner = slice(16, 16 + size_y)
    put(wide, slice(8, 8 + size_x), inner, own[...])
    near_at = (size_x + 8) * (1 - par_x)
    far_at = (size_x + 8) * par_x
    put(wide, pl.ds(near_at, 8), inner, near[0:8])
    put(wide, pl.ds(far_at, 8), inner, far[0:8])
    for side in range(2):
        rows = slice(8, 16) if side == 0 else slice(16 + size_y, 24 + size_y)

        def fill(which, rows=rows):
            if which < len(strips):
                put(wide, slice(8, 8 + size_x), rows, strips[which][8 * first : 8 * first + 8])
                put(wide, pl.ds(near_at, 8), rows, near_strips[which][8 * first : 8 * first + 8])
                corner_at = 4 + (size_x + 4) * par_x
                put(wide, pl.ds(corner_at, 4), rows, corners[which][4 * first : 4 * first + 4])
            else:
                zero = jnp.zeros((size_x + 8, 8, 2 * LANES), F32)
                put(wide, slice(4, 12 + size_x), rows, zero)

        pl.when(par_y == 1 - side)(functools.partial(fill, 0))
        pl.when(par_y == side)(functools.partial(fill, 1))


def each_side(scalars, count, size_y, present, absent):
    par_y = scalars[1]
    for side in range(2):
        start = 0 if side == 0 else 8 + size_y
        for which in range(2):
            action = present if which < count else absent
            at = 1 - side if which == 0 else side
            pl.when(par_y == at)(functools.partial(action, start))


def send_strips(scalars, value, size_x, size_y):
    even = scalars[1] == 0
    low = value[:, 0:8, :]
    high = value[:, size_y - 8 : size_y, :]
    return [jnp.where(even, high, low), jnp.where(even, low, high)]


def step_pair_kernel(count, tangent, blank, at, *refs):
    refs = list(refs)
    scalars = parity()
    if not tangent:
        sems, source, wave = refs.pop(), refs.pop(-2), refs.pop()
        small = [
            pltpu.make_async_copy(refs[0], source, sems.at[0]),
            pltpu.make_async_copy(refs[1], wave, sems.at[1]),
        ]
        for copy in small:
            copy.start()
        refs = refs[2:]
    if not blank:
        own, near, far = refs[:3]
        refs = refs[3:]
        strips, refs = refs[:count], refs[count:]
        near_strips, refs = refs[:count], refs[count:]
        corners, refs = refs[:count], refs[count:]
        prev = refs.pop(0)
    speed = refs.pop(0)
    if tangent:
        drive1, drive2 = refs[:2]
        refs = refs[2:]
        partner_strips, refs = refs[:count], refs[count:]
    else:
        perturb = refs.pop(0)
    next1, next2 = refs[:2]
    refs = refs[2:]
    if not tangent:
        drive1, drive2 = refs[:2]
        refs = refs[2:]
    strip_out, refs = refs[:count], refs[count:]
    if tangent:
        corner_out, refs = refs[:count], refs[count:]
    size_x, size_y, _ = next2.shape
    par_x = scalars[0]
    inner = slice(8, 8 + size_y)

    def lanes(rows):
        return lax.broadcasted_iota(jnp.int32, (rows, LANES), 1)

    if not blank:
        wide = refs.pop(0)
        place_wide(
            wide, scalars, own, near, far, strips, near_strips, corners, 1 if tangent else 0
        )

        def advance(layer, start, rows):
            laps = laplace(wide, layer + 4, start + 8, rows, lanes(rows))
            span = slice(start, start + rows)
            for half in range(2):
                value = wide[layer + 4, half, start + 8 : start + 8 + rows, :]
                fresh = (
                    2.0 * value
                    - prev[layer, half, span, :]
                    + speed[layer, half, span, :] * laps[half]
                )
                if tangent:
                    fresh = fresh + drive1[layer, half, span, :]
                else:
                    drive1[layer, half, span, :] = perturb[layer, half, span, :] * laps[half]
                next1[layer, half, span, :] = fresh

        for layer in range(size_x + 8):
            advance(layer, 8, size_y)

        def present(start):
            for layer in range(4, 4 + size_x):
                advance(layer, start, 8)

        def absent(start):
            zero = jnp.zeros((size_x, 2, 8, LANES), F32)
            next1[4 : 4 + size_x, :, start : start + 8, :] = zero
            if not tangent:
                drive1[4 : 4 + size_x, :, start : start + 8, :] = zero

        each_side(scalars, count, size_y, present, absent)
    else:
        next1[...] = drive1[...]

    if not tangent:
        for copy in small:
            copy.wait()
        src_x = source[0] - lax.axis_index("gx") * size_x
        src_y = source[1] - lax.axis_index("gy") * size_y
        src_z = source[2]

        @pl.when((src_x >= -4) & (src_x < size_x + 4) & (src_y >= -8) & (src_y < size_y + 8))
        def _():
            half = lax.shift_right_logical(src_z, 7)
            hit = lax.broadcasted_iota(jnp.int32, (1, LANES), 1) == src_z - half * LANES
            row = next1[src_x + 4, half, pl.ds(src_y + 8, 1), :]
            next1[src_x + 4, half, pl.ds(src_y + 8, 1), :] = row + jnp.where(hit, wave[at], 0.0)

    for layer in range(size_x):
        laps = laplace(next1, layer + 4, 8, size_y, lanes(size_y))
        for half in range(2):
            fresh = 2.0 * next1[layer + 4, half, inner, :]
            if not blank:
                fresh = fresh - wide[layer + 8, half, 16 : 16 + size_y, :]
            fresh = fresh + speed[layer + 4, half, inner, :] * laps[half]
            if tangent:
                fresh = fresh + drive2[layer, half]
            else:
                drive2[layer, half] = perturb[layer + 4, half, inner, :] * laps[half]
            next2[layer, :, half * LANES : (half + 1) * LANES] = fresh

    if not tangent:

        @pl.when((src_x >= 0) & (src_x < size_x) & (src_y >= 0) & (src_y < size_y))
        def _():
            hit = lax.broadcasted_iota(jnp.int32, (1, 2 * LANES), 1) == src_z
            row = next2[src_x, pl.ds(src_y, 1), :]
            next2[src_x, pl.ds(src_y, 1), :] = row + jnp.where(hit, wave[at + 1], 0.0)

    made = send_strips(scalars, next2[...], size_x, size_y)
    for which in range(count):
        if not tangent:
            strip_out[which][...] = made[which]
        else:
            strip_out[which][0:size_x] = partner_strips[which][...]
            strip_out[which][size_x : 2 * size_x] = made[which]
            facing = pl.ds((size_x - 4) * par_x, 4)
            corner_out[which][0:4] = partner_strips[which][facing]
            strip = strip_out[which][pl.ds(size_x + (size_x - 4) * par_x, 4)]
            corner_out[which][4:8] = strip


def wide_shape(shape):
    return pltpu.VMEM((shape[0] + 16, 2, shape[1] + 32, LANES), F32)


def ring_struct(shape):
    return struct(shape[0] + 8, 2, shape[1] + 16, LANES)


def pressure_steps(shape, count, at, source, wave, pieces, prev, speed, perturb):
    own, near, far, strips, near_strips, corners = pieces
    outs = [ring_struct(shape), struct(*shape), ring_struct(shape)]
    outs += [struct(shape[0], 2, shape[1], LANES)]
    outs += [struct(shape[0], 8, shape[2])] * count
    args = [own, near, far, *strips, *near_strips, *corners, prev, speed, perturb]
    out = pl.pallas_call(
        functools.partial(step_pair_kernel, count, False, False, at),
        out_shape=outs,
        in_specs=[pl.BlockSpec(memory_space=pl.ANY)] * 2 + [VMEM] * len(args),
        out_specs=[VMEM] * len(outs),
        scratch_shapes=[
            wide_shape(shape),
            pltpu.SMEM(source.shape, jnp.int32),
            pltpu.SMEM(wave.shape, F32),
            pltpu.SemaphoreType.DMA((2,)),
        ],
        compiler_params=params(),
        cost_estimate=cost(900_000_000, 400_000_000),
        name="pressure_steps",
    )(source, wave, *args)
    return out[0], out[1], out[2], out[3], list(out[4:])


def tangent_steps(shape, count, pieces, prev, speed, drive1, drive2, partner_strips):
    blank = pieces is None
    outs = [ring_struct(shape), struct(*shape)]
    outs += [struct(2 * shape[0], 8, shape[2])] * count
    outs += [struct(8, 8, shape[2])] * count
    args = []
    if not blank:
        own, near, far, strips, near_strips, corners = pieces
        args = [own, near, far, *strips, *near_strips, *corners, prev]
    args += [speed, drive1, drive2, *partner_strips]
    out = pl.pallas_call(
        functools.partial(step_pair_kernel, count, True, blank, 0),
        out_shape=outs,
        in_specs=[VMEM] * len(args),
        out_specs=[VMEM] * len(outs),
        scratch_shapes=[] if blank else [wide_shape(shape)],
        compiler_params=params(),
        cost_estimate=cost(900_000_000, 400_000_000),
        name="tangent_steps",
    )(*args)
    return out[0], out[1], list(out[2 : 2 + count]), list(out[2 + count :])


def pack_kernel(count, p_now, p_prev, speed, perturb, far, near, *rest):
    size_x, size_y, _ = p_now.shape
    strips, corners, sems = rest[:count], rest[count : 2 * count], rest[2 * count]
    par_x, par_y = parity()
    far_face = pl.ds((size_x - 4) * par_x, 4)
    near_face = pl.ds((size_x - 4) * (1 - par_x), 4)
    moves = []
    for target, face in ((far, far_face), (near, near_face)):
        for k, field in enumerate((p_prev, speed, perturb)):
            start = 4 * k
            moves.append((field.at[face], target.at[start : start + 4]))
    for which in range(count):
        high = 1 - par_y if which == 0 else par_y
        rows = pl.ds(pl.multiple_of(high * (size_y - 8), 8), 8)
        for k, field in enumerate((p_now, perturb, p_prev, speed)):
            moves.append((field.at[:, rows], strips[which].at[k * size_x : (k + 1) * size_x]))
            if k < 2:
                moves.append((field.at[far_face, rows], corners[which].at[4 * k : 4 * k + 4]))
    copies = [
        pltpu.make_async_copy(source, target, sems.at[k]) for k, (source, target) in enumerate(moves)
    ]
    for copy in copies:
        copy.start()
    for copy in copies:
        copy.wait()


def pack(shape, count, p_now, p_prev, speed, perturb):
    outs = [struct(12, shape[1], shape[2])] * 2
    outs += [struct(4 * shape[0], 8, shape[2])] * count
    outs += [struct(8, 8, shape[2])] * count
    out = pl.pallas_call(
        functools.partial(pack_kernel, count),
        out_shape=outs,
        in_specs=[pl.BlockSpec(memory_space=pl.ANY)] * 4,
        out_specs=[VMEM] * len(outs),
        scratch_shapes=[pltpu.SemaphoreType.DMA((6 + 6 * count,))],
        compiler_params=pltpu.CompilerParams(vmem_limit_bytes=58 * 1024 * 1024),
        cost_estimate=cost(10_000, 3_000_000),
        name="pack",
    )(p_now, p_prev, speed, perturb)
    return out[0], out[1], list(out[2 : 2 + count]), list(out[2 + count :])


def gather_ring_kernel(count, p_prev, speed, perturb, near, far, _, *refs):
    strips, refs = refs[:count], refs[count:]
    near_strips, refs = refs[:count], refs[count:]
    corners, targets = refs[:count], refs[count:]
    size_x, size_y, _ = p_prev.shape
    par_x, par_y = parity()
    inner = slice(8, 8 + size_y)
    near_at = (size_x + 4) * (1 - par_x)
    far_at = (size_x + 4) * par_x
    for k, (own, target) in enumerate(zip((p_prev, speed, perturb), targets)):
        put(target, slice(4, 4 + size_x), inner, own[...])
        face = slice(4 * k, 4 * k + 4)
        put(target, pl.ds(near_at, 4), inner, near[face])
        put(target, pl.ds(far_at, 4), inner, far[face])
        part = (2, 3, 1)[k]
        for side in range(2):
            rows = slice(0, 8) if side == 0 else slice(8 + size_y, 16 + size_y)

            def fill(which, k=k, rows=rows, target=target, part=part):
                if which < count:
                    base = part * size_x
                    put(target, slice(4, 4 + size_x), rows, strips[which][base : base + size_x])
                    if k == 2:
                        face = pl.ds(base + (size_x - 4) * par_x, 4)
                        put(target, pl.ds(near_at, 4), rows, near_strips[which][face])
                        put(target, pl.ds(far_at, 4), rows, corners[which][4:8])
                else:
                    zero = jnp.zeros((size_x + 8, 8, 2 * LANES), F32)
                    put(target, slice(0, 8 + size_x), rows, zero)

            pl.when(par_y == 1 - side)(functools.partial(fill, 0))
            pl.when(par_y == side)(functools.partial(fill, 1))


def gather_ring(shape, count, fields, near, far, p_far, strips, near_strips, corners):
    args = [*fields, near, far, p_far, *strips, *near_strips, *corners]
    return pl.pallas_call(
        functools.partial(gather_ring_kernel, count),
        out_shape=[ring_struct(shape)] * 3,
        in_specs=[VMEM] * len(args),
        out_specs=[VMEM] * 3,
        compiler_params=params(),
        cost_estimate=cost(10_000, 4_000_000),
        name="gather_ring",
    )(*args)


def receive_kernel(rounds, cells, p1, p2, q1, q2, *refs):
    size_x, size_y, size_z = p2.shape
    if rounds == 0:
        observed, refs = refs[0], refs[1:]
        refs[2][...] = observed[...]
        synth, born = refs[:2]
    elif rounds > 0:
        earlier, observed = refs[: 2 * rounds], refs[2 * rounds]
        synth, born, spread = refs[2 * rounds + 1 :]
    else:
        synth, born = refs
    steps = synth.shape[0]
    rows, count = size_x * size_y, cells.shape[1]
    flat = cells[...]
    shift = size_z.bit_length() - 1
    row_of = lax.shift_right_logical(flat, shift)
    depth_of = flat - lax.shift_left(row_of, shift)
    pick = lax.broadcasted_iota(jnp.int32, (rows, count), 0) == row_of
    pick = pick.astype(F32).astype(jnp.bfloat16)
    depth = lax.broadcasted_iota(jnp.int32, (LANES, count), 0)
    hits = [depth == depth_of, depth + LANES == depth_of]

    def at(parts):
        total = jnp.zeros((1, count), F32)
        for part, hit in zip(parts, hits):
            rest = part
            picked = None
            for _ in range(3):
                piece = rest.astype(jnp.bfloat16)
                rest = rest - piece.astype(F32)
                got = lax.dot_general(
                    piece, pick, (((0,), (0,)), ((), ())), preferred_element_type=F32
                )
                picked = got if picked is None else picked + got
            total = total + jnp.sum(jnp.where(hit, picked, 0.0), axis=0, keepdims=True)
        return total

    for one, two, target in ((p1, p2, synth), (q1, q2, born)):
        first = [
            one[4 : 4 + size_x, half, 8 : 8 + size_y, :].reshape(rows, LANES) for half in range(2)
        ]
        target[steps - 2 : steps - 1, :] = at(first)
        second = [part.reshape(rows, LANES) for part in halves(two[...])]
        target[steps - 1 : steps, :] = at(second)


    if rounds > 0:
        for k in range(rounds):
            synth[2 * k : 2 * k + 2, :] = earlier[2 * k][...]
            born[2 * k : 2 * k + 2, :] = earlier[2 * k + 1][...]
        residual = observed[...] - synth[...]
        tangent = born[...]
        synth[...] = residual
        numer, denom = jnp.sum(residual * tangent), jnp.sum(tangent * tangent)
        lane = lax.broadcasted_iota(jnp.int32, spread.shape, 2)
        spread[...] = jnp.where(lane == 0, numer, jnp.where(lane == 1, denom, 0.0))


def receive(cells, p1, p2, q1, q2, earlier=(), observed=None, total=0):
    count = cells.shape[1]
    rounds = len(earlier) // 2 if total else (-1 if observed is None else 0)
    outs = [struct(2 * max(rounds, 0) + 2, count)] * 2
    args = [cells, p1, p2, q1, q2]
    if rounds == 0:
        outs.append(struct(*observed.shape))
        args.append(observed)
    elif rounds > 0:
        outs.append(struct(total, 1, LANES))
        args += [*earlier, observed]
    return pl.pallas_call(
        functools.partial(receive_kernel, rounds),
        out_shape=outs,
        in_specs=[VMEM] * len(args),
        out_specs=[VMEM] * len(outs),
        compiler_params=params(),
        cost_estimate=cost(20_000_000, 2_500_000),
        name="receive",
    )(*args)


def finish_kernel(sums, residual, born, speed, smooth, predicted, model, traces, field, sems):
    lane = lax.broadcasted_iota(jnp.int32, sums.shape, 2)
    values = sums[...]
    numer = jnp.sum(jnp.where(lane == 0, values, 0.0))
    denom = jnp.sum(jnp.where(lane == 1, values, 0.0))
    length = jnp.full((1, LANES), numer) / (jnp.full((1, LANES), denom) + 1e-6)
    traces[...] = residual[...] - length * born[...]
    first = pltpu.make_async_copy(traces, predicted, sems.at[0])
    first.start()
    both = jnp.concatenate([length, length], axis=1)
    field[...] = speed[...] + both[None] * smooth[...]
    second = pltpu.make_async_copy(field, model, sems.at[1])
    second.start()
    first.wait()
    second.wait()


def finish(sums, residual, born, speed, smooth):
    outs = [struct(*born.shape), struct(*speed.shape)]
    return pl.pallas_call(
        finish_kernel,
        out_shape=outs,
        in_specs=[VMEM] * 5,
        out_specs=[pl.BlockSpec(memory_space=pl.ANY)] * 2,
        scratch_shapes=[
            pltpu.VMEM(born.shape, F32),
            pltpu.VMEM(speed.shape, F32),
            pltpu.SemaphoreType.DMA((2,)),
        ],
        compiler_params=params(),
        cost_estimate=cost(200_000, 800_000),
        name="finish",
    )(sums, residual, born, speed, smooth)


def smooth_kernel(perturb, p_in, q_in, smooth, p_out, q_out, sems):
    copies = [
        pltpu.make_async_copy(p_in, p_out, sems.at[0]),
        pltpu.make_async_copy(q_in, q_out, sems.at[1]),
    ]
    for copy in copies:
        copy.start()
    size_x, size_y, _ = smooth.shape
    lane = lax.broadcasted_iota(jnp.int32, (size_y, LANES), 1)

    def layer_step(layer, carry):
        parts = []
        for half in range(2):

            def along_x(start, half=half):
                span = slice(start, start + size_y)
                return (
                    0.25 * perturb[layer + 3, half, span, :]
                    + 0.5 * perturb[layer + 4, half, span, :]
                    + 0.25 * perturb[layer + 5, half, span, :]
                )

            parts.append(0.25 * along_x(7) + 0.5 * along_x(8) + 0.25 * along_x(9))
        up = [pltpu.roll(value, LANES - 1, 1) for value in parts]
        down = [pltpu.roll(value, 1, 1) for value in parts]
        keep_up, keep_down = lane < LANES - 1, lane >= 1
        above = [jnp.where(keep_up, up[0], up[1]), jnp.where(keep_up, up[1], 0.0)]
        below = [jnp.where(keep_down, down[0], 0.0), jnp.where(keep_down, down[1], down[0])]
        for half in range(2):
            value = 0.25 * below[half] + 0.5 * parts[half] + 0.25 * above[half]
            smooth[layer, :, half * LANES : (half + 1) * LANES] = value
        return carry

    lax.fori_loop(0, size_x, layer_step, 0)
    for copy in copies:
        copy.wait()


def smoothed(shape, perturb, p_now, q_now):
    return pl.pallas_call(
        smooth_kernel,
        out_shape=[struct(*shape)] * 3,
        in_specs=[VMEM] * 3,
        out_specs=[VMEM] + [pl.BlockSpec(memory_space=pl.ANY)] * 2,
        scratch_shapes=[pltpu.SemaphoreType.DMA((2,))],
        compiler_params=params(),
        cost_estimate=cost(1_000_000, 2_200_000),
        name="smooth",
    )(perturb, p_now, q_now)


def on_device(
    pressure_prev, pressure_now, courant, perturbation, source_pos, wavelet, rec_cells, observed
):
    shape = pressure_now.shape
    size_x, size_y, size_z = shape
    count_x, count_y = lax.axis_size("gx"), lax.axis_size("gy")
    steps = wavelet.shape[0]
    near_x, far_x = near_pairs(count_x), far_pairs(count_x)
    pairs_y = [near_pairs(count_y)]
    if count_y > 2:
        pairs_y.append(far_pairs(count_y))
    count = len(pairs_y)
    far_diagonal = [diagonal(far_x, pairs, count_y) for pairs in pairs_y]

    def swap_near(value):
        return lax.ppermute(value, "gx", near_x)

    def swap_far(value):
        return lax.ppermute(value, "gx", far_x)

    def swap_strips(strips, corners):
        got = [lax.ppermute(value, "gy", pairs) for value, pairs in zip(strips, pairs_y)]
        got_corners = [
            lax.ppermute(value, AXES, pairs) for value, pairs in zip(corners, far_diagonal)
        ]
        return got, [swap_near(value) for value in got], got_corners

    p_far, p_near = swap_far(pressure_now), swap_near(pressure_now)
    far_send, near_send, strips, corners = pack(
        shape, count, pressure_now, pressure_prev, courant, perturbation
    )
    far, near = swap_far(far_send), swap_near(near_send)
    strips, near_strips, corners = swap_strips(strips, corners)
    p_prev, speed, perturb = gather_ring(
        shape,
        count,
        (pressure_prev, courant, perturbation),
        near,
        far,
        p_far,
        strips,
        near_strips,
        corners,
    )
    cells = rec_cells.reshape(1, -1)
    p_cur, q_cur, q_prev = pressure_now, None, None
    q_far = q_near = None
    earlier = []
    traces = observed.reshape(steps, -1)
    for step in range(0, steps, 2):
        around = (strips, near_strips, corners)
        p_pieces = (p_cur, p_near, p_far) + around
        q_pieces = None if q_cur is None else (q_cur, q_near, q_far) + around
        p_prev, p_cur, drive1, drive2, p_strips = pressure_steps(
            shape, count, step, source_pos, wavelet, p_pieces, p_prev, speed, perturb
        )
        last = step + 2 >= steps
        if not last:
            p_far, p_near = swap_far(p_cur), swap_near(p_cur)
        q_prev, q_cur, strips, corners = tangent_steps(
            shape, count, q_pieces, q_prev, speed, drive1, drive2, p_strips
        )
        if not last:
            strips, near_strips, corners = swap_strips(strips, corners)
            q_far, q_near = swap_far(q_cur), swap_near(q_cur)
        if not last:
            got = list(receive(cells, p_prev, p_cur, q_prev, q_cur, (), traces))
            if step == 0:
                held = got.pop()
            traces = None
            earlier += got
    total = count_x * count_y
    residual, born, spread = receive(
        cells, p_prev, p_cur, q_prev, q_cur, earlier, held, total
    )
    sums = lax.all_to_all(spread, AXES, 0, 0)
    smooth, p_cur, q_cur = smoothed(shape, perturb, p_cur, q_cur)
    predicted, updated_model = finish(sums, residual, born, courant, smooth)
    predicted = predicted.reshape(observed.shape)
    return (p_cur, q_cur, predicted, updated_model)


def solution(mesh):
    field = P("gx", "gy", None)
    traces = P("gx", "gy", None, None)
    return jax.shard_map(
        on_device,
        mesh=mesh,
        in_specs=(field, field, field, field, P(), P(), field, traces),
        out_specs=(field, field, traces, field),
        check_vma=False,
    )
```

```python
import functools

import jax
import jax.numpy as jnp
from jax import lax
from jax.experimental import pallas as pl
from jax.experimental.pallas import tpu as pltpu
from jax.sharding import PartitionSpec as P

COEF = (-205.0 / 72.0, 8.0 / 5.0, -1.0 / 5.0, 8.0 / 315.0, -1.0 / 560.0)
AXES = ("gx", "gy")
LANES = 128
F32 = jnp.float32

VMEM = pl.BlockSpec(memory_space=pltpu.VMEM)


def struct(*shape):
    return jax.ShapeDtypeStruct(shape, F32)


def params():
    return pltpu.CompilerParams(vmem_limit_bytes=24 * 1024 * 1024)


def cost(flops, moved):
    return pl.CostEstimate(flops=flops, bytes_accessed=moved, transcendentals=0)


def near_pairs(count):
    return [(i, i ^ 1) for i in range(count)]


def far_pairs(count):
    pairs = []
    for i in range(1, count - 1, 2):
        pairs += [(i, i + 1), (i + 1, i)]
    return pairs


def diagonal(pairs_x, pairs_y, count_y):
    return [(a * count_y + b, c * count_y + d) for a, c in pairs_x for b, d in pairs_y]


def parity():
    return lax.rem(lax.axis_index("gx"), 2), lax.rem(lax.axis_index("gy"), 2)


def laplace(field, layer, row, rows, lane):
    centre = [field[layer, half, row : row + rows, :] for half in range(2)]
    totals = [(3.0 * COEF[0]) * value for value in centre]
    for k in range(1, 5):
        keep_up = lane < LANES - k
        keep_down = lane >= k
        up = [pltpu.roll(value, LANES - k, 1) for value in centre]
        down = [pltpu.roll(value, k, 1) for value in centre]
        depth = [
            jnp.where(keep_up, up[0], up[1]) + jnp.where(keep_down, down[0], 0.0),
            jnp.where(keep_up, up[1], 0.0) + jnp.where(keep_down, down[1], down[0]),
        ]
        for half in range(2):
            pair = (
                field[layer + k, half, row : row + rows, :]
                + field[layer - k, half, row : row + rows, :]
            )
            pair = pair + (
                field[layer, half, row + k : row + k + rows, :]
                + field[layer, half, row - k : row - k + rows, :]
            )
            totals[half] = totals[half] + COEF[k] * (pair + depth[half])
    return totals


def halves(value):
    return (value[..., :LANES], value[..., LANES:])


def put(target, layers, rows, value):
    for half, part in enumerate(halves(value)):
        target[layers, half, rows, :] = part


def place_wide(wide, scalars, own, near, far, strips, near_strips, corners, first):
    size_x, size_y, _ = own.shape
    par_x = scalars[0]
    par_y = scalars[1]
    inner = slice(16, 16 + size_y)
    put(wide, slice(8, 8 + size_x), inner, own[...])
    near_at = (size_x + 8) * (1 - par_x)
    far_at = (size_x + 8) * par_x
    put(wide, pl.ds(near_at, 8), inner, near[0:8])
    put(wide, pl.ds(far_at, 8), inner, far[0:8])
    for side in range(2):
        rows = slice(8, 16) if side == 0 else slice(16 + size_y, 24 + size_y)

        def fill(which, rows=rows):
            if which < len(strips):
                put(wide, slice(8, 8 + size_x), rows, strips[which][8 * first : 8 * first + 8])
                put(wide, pl.ds(near_at, 8), rows, near_strips[which][8 * first : 8 * first + 8])
                corner_at = 4 + (size_x + 4) * par_x
                put(wide, pl.ds(corner_at, 4), rows, corners[which][4 * first : 4 * first + 4])
            else:
                zero = jnp.zeros((size_x + 8, 8, 2 * LANES), F32)
                put(wide, slice(4, 12 + size_x), rows, zero)

        pl.when(par_y == 1 - side)(functools.partial(fill, 0))
        pl.when(par_y == side)(functools.partial(fill, 1))


def each_side(scalars, count, size_y, present, absent):
    par_y = scalars[1]
    for side in range(2):
        start = 0 if side == 0 else 8 + size_y
        for which in range(2):
            action = present if which < count else absent
            at = 1 - side if which == 0 else side
            pl.when(par_y == at)(functools.partial(action, start))


def send_strips(scalars, value, size_x, size_y):
    even = scalars[1] == 0
    low = value[:, 0:8, :]
    high = value[:, size_y - 8 : size_y, :]
    return [jnp.where(even, high, low), jnp.where(even, low, high)]


def step_pair_kernel(count, tangent, blank, at, *refs):
    refs = list(refs)
    scalars = parity()
    if not tangent:
        sems, source, wave = refs.pop(), refs.pop(-2), refs.pop()
        small = [
            pltpu.make_async_copy(refs[0], source, sems.at[0]),
            pltpu.make_async_copy(refs[1], wave, sems.at[1]),
        ]
        for copy in small:
            copy.start()
        refs = refs[2:]
    if tangent and not blank:
        wide, prev = refs[:2]
        refs = refs[2:]
    elif not blank:
        own, near, far = refs[:3]
        refs = refs[3:]
        strips, refs = refs[:count], refs[count:]
        near_strips, refs = refs[:count], refs[count:]
        corners, refs = refs[:count], refs[count:]
        prev = refs.pop(0)
    speed = refs.pop(0)
    if tangent:
        drive1, drive2 = refs[:2]
        refs = refs[2:]
        partner_strips, refs = refs[:count], refs[count:]
    else:
        perturb = refs.pop(0)
    next1, next2 = refs[:2]
    refs = refs[2:]
    if not tangent:
        drive1, drive2 = refs[:2]
        refs = refs[2:]
    strip_out, refs = refs[:count], refs[count:]
    if tangent:
        corner_out, refs = refs[:count], refs[count:]
    size_x, size_y, _ = next2.shape
    par_x = scalars[0]
    inner = slice(8, 8 + size_y)

    def lanes(rows):
        return lax.broadcasted_iota(jnp.int32, (rows, LANES), 1)

    if not blank:
        if not tangent:
            wide = refs.pop(0)
            place_wide(wide, scalars, own, near, far, strips, near_strips, corners, 0)

        def advance(layer, start, rows):
            laps = laplace(wide, layer + 4, start + 8, rows, lanes(rows))
            span = slice(start, start + rows)
            for half in range(2):
                value = wide[layer + 4, half, start + 8 : start + 8 + rows, :]
                fresh = (
                    2.0 * value
                    - prev[layer, half, span, :]
                    + speed[layer, half, span, :] * laps[half]
                )
                if tangent:
                    fresh = fresh + drive1[layer, half, span, :]
                else:
                    drive1[layer, half, span, :] = perturb[layer, half, span, :] * laps[half]
                next1[layer, half, span, :] = fresh

        for layer in range(size_x + 8):
            advance(layer, 8, size_y)

        def present(start):
            for layer in range(4, 4 + size_x):
                advance(layer, start, 8)

        def absent(start):
            zero = jnp.zeros((size_x, 2, 8, LANES), F32)
            next1[4 : 4 + size_x, :, start : start + 8, :] = zero
            if not tangent:
                drive1[4 : 4 + size_x, :, start : start + 8, :] = zero

        each_side(scalars, count, size_y, present, absent)
    else:
        next1[...] = drive1[...]

    if not tangent:
        for copy in small:
            copy.wait()
        src_x = source[0] - lax.axis_index("gx") * size_x
        src_y = source[1] - lax.axis_index("gy") * size_y
        src_z = source[2]

        @pl.when((src_x >= -4) & (src_x < size_x + 4) & (src_y >= -8) & (src_y < size_y + 8))
        def _():
            half = lax.shift_right_logical(src_z, 7)
            hit = lax.broadcasted_iota(jnp.int32, (1, LANES), 1) == src_z - half * LANES
            row = next1[src_x + 4, half, pl.ds(src_y + 8, 1), :]
            next1[src_x + 4, half, pl.ds(src_y + 8, 1), :] = row + jnp.where(hit, wave[at], 0.0)

    for layer in range(size_x):
        laps = laplace(next1, layer + 4, 8, size_y, lanes(size_y))
        for half in range(2):
            fresh = 2.0 * next1[layer + 4, half, inner, :]
            if not blank:
                fresh = fresh - wide[layer + 8, half, 16 : 16 + size_y, :]
            fresh = fresh + speed[layer + 4, half, inner, :] * laps[half]
            if tangent:
                fresh = fresh + drive2[layer, half]
            else:
                drive2[layer, half] = perturb[layer + 4, half, inner, :] * laps[half]
            next2[layer, :, half * LANES : (half + 1) * LANES] = fresh

    if not tangent:

        @pl.when((src_x >= 0) & (src_x < size_x) & (src_y >= 0) & (src_y < size_y))
        def _():
            hit = lax.broadcasted_iota(jnp.int32, (1, 2 * LANES), 1) == src_z
            row = next2[src_x, pl.ds(src_y, 1), :]
            next2[src_x, pl.ds(src_y, 1), :] = row + jnp.where(hit, wave[at + 1], 0.0)

    made = send_strips(scalars, next2[...], size_x, size_y)
    for which in range(count):
        if not tangent:
            strip_out[which][...] = made[which]
        else:
            strip_out[which][0:size_x] = partner_strips[which][...]
            strip_out[which][size_x : 2 * size_x] = made[which]
            facing = pl.ds((size_x - 4) * par_x, 4)
            corner_out[which][0:4] = partner_strips[which][facing]
            strip = strip_out[which][pl.ds(size_x + (size_x - 4) * par_x, 4)]
            corner_out[which][4:8] = strip


def place_kernel(count, own, near, far, *refs):
    strips, near_strips, corners = (refs[k * count : (k + 1) * count] for k in range(3))
    place_wide(refs[-1], parity(), own, near, far, strips, near_strips, corners, 1)


def wide_shape(shape):
    return pltpu.VMEM((shape[0] + 16, 2, shape[1] + 32, LANES), F32)


def ring_struct(shape):
    return struct(shape[0] + 8, 2, shape[1] + 16, LANES)


def pressure_steps(shape, count, at, source, wave, pieces, prev, speed, perturb):
    own, near, far, strips, near_strips, corners = pieces
    outs = [ring_struct(shape), struct(*shape), ring_struct(shape)]
    outs += [struct(shape[0], 2, shape[1], LANES)]
    outs += [struct(shape[0], 8, shape[2])] * count
    args = [own, near, far, *strips, *near_strips, *corners, prev, speed, perturb]
    out = pl.pallas_call(
        functools.partial(step_pair_kernel, count, False, False, at),
        out_shape=outs,
        in_specs=[pl.BlockSpec(memory_space=pl.ANY)] * 2 + [VMEM] * len(args),
        out_specs=[VMEM] * len(outs),
        scratch_shapes=[
            wide_shape(shape),
            pltpu.SMEM(source.shape, jnp.int32),
            pltpu.SMEM(wave.shape, F32),
            pltpu.SemaphoreType.DMA((2,)),
        ],
        compiler_params=params(),
        cost_estimate=cost(900_000_000, 400_000_000),
        name="pressure_steps",
    )(source, wave, *args)
    return out[0], out[1], out[2], out[3], list(out[4:])


def tangent_steps(shape, count, pieces, prev, speed, drive1, drive2, partner_strips):
    blank = pieces is None
    outs = [ring_struct(shape), struct(*shape)]
    outs += [struct(2 * shape[0], 8, shape[2])] * count
    outs += [struct(8, 8, shape[2])] * count
    args = []
    if not blank:
        own, near, far, strips, near_strips, corners, done = pieces
        args = [own, near, far, *strips, *near_strips, *corners, done]
        wide = pl.pallas_call(
            functools.partial(place_kernel, count),
            out_shape=struct(shape[0] + 16, 2, shape[1] + 32, LANES),
            in_specs=[VMEM] * len(args),
            out_specs=VMEM,
            compiler_params=params(),
            cost_estimate=cost(10_000, 3_000_000),
            name="place",
        )(*args)
        args = [wide, prev]
    args += [speed, drive1, drive2, *partner_strips]
    out = pl.pallas_call(
        functools.partial(step_pair_kernel, count, True, blank, 0),
        out_shape=outs,
        in_specs=[VMEM] * len(args),
        out_specs=[VMEM] * len(outs),
        compiler_params=params(),
        cost_estimate=cost(900_000_000, 400_000_000),
        name="tangent_steps",
    )(*args)
    return out[0], out[1], list(out[2 : 2 + count]), list(out[2 + count :])


def pack_kernel(count, p_now, p_prev, speed, perturb, far, near, *rest):
    size_x, size_y, _ = p_now.shape
    strips, corners, sems = rest[:count], rest[count : 2 * count], rest[2 * count]
    par_x, par_y = parity()
    far_face = pl.ds((size_x - 4) * par_x, 4)
    near_face = pl.ds((size_x - 4) * (1 - par_x), 4)
    moves = []
    for target, face in ((far, far_face), (near, near_face)):
        for k, field in enumerate((p_prev, speed, perturb)):
            start = 4 * k
            moves.append((field.at[face], target.at[start : start + 4]))
    for which in range(count):
        high = 1 - par_y if which == 0 else par_y
        rows = pl.ds(pl.multiple_of(high * (size_y - 8), 8), 8)
        for k, field in enumerate((p_now, perturb, p_prev, speed)):
            moves.append((field.at[:, rows], strips[which].at[k * size_x : (k + 1) * size_x]))
            if k < 2:
                moves.append((field.at[far_face, rows], corners[which].at[4 * k : 4 * k + 4]))
    copies = [
        pltpu.make_async_copy(source, target, sems.at[k]) for k, (source, target) in enumerate(moves)
    ]
    for copy in copies:
        copy.start()
    for copy in copies:
        copy.wait()


def pack(shape, count, p_now, p_prev, speed, perturb):
    outs = [struct(12, shape[1], shape[2])] * 2
    outs += [struct(4 * shape[0], 8, shape[2])] * count
    outs += [struct(8, 8, shape[2])] * count
    out = pl.pallas_call(
        functools.partial(pack_kernel, count),
        out_shape=outs,
        in_specs=[pl.BlockSpec(memory_space=pl.ANY)] * 4,
        out_specs=[VMEM] * len(outs),
        scratch_shapes=[pltpu.SemaphoreType.DMA((6 + 6 * count,))],
        compiler_params=pltpu.CompilerParams(vmem_limit_bytes=58 * 1024 * 1024),
        cost_estimate=cost(10_000, 3_000_000),
        name="pack",
    )(p_now, p_prev, speed, perturb)
    return out[0], out[1], list(out[2 : 2 + count]), list(out[2 + count :])


def gather_ring_kernel(count, p_prev, speed, perturb, near, far, *refs):
    strips, refs = refs[:count], refs[count:]
    near_strips, refs = refs[:count], refs[count:]
    corners, targets = refs[:count], refs[count:]
    size_x, size_y, _ = p_prev.shape
    par_x, par_y = parity()
    inner = slice(8, 8 + size_y)
    near_at = (size_x + 4) * (1 - par_x)
    far_at = (size_x + 4) * par_x
    for k, (own, target) in enumerate(zip((p_prev, speed, perturb), targets)):
        put(target, slice(4, 4 + size_x), inner, own[...])
        face = slice(4 * k, 4 * k + 4)
        put(target, pl.ds(near_at, 4), inner, near[face])
        put(target, pl.ds(far_at, 4), inner, far[face])
        part = (2, 3, 1)[k]
        for side in range(2):
            rows = slice(0, 8) if side == 0 else slice(8 + size_y, 16 + size_y)

            def fill(which, k=k, rows=rows, target=target, part=part):
                if which < count:
                    base = part * size_x
                    put(target, slice(4, 4 + size_x), rows, strips[which][base : base + size_x])
                    if k == 2:
                        face = pl.ds(base + (size_x - 4) * par_x, 4)
                        put(target, pl.ds(near_at, 4), rows, near_strips[which][face])
                        put(target, pl.ds(far_at, 4), rows, corners[which][4:8])
                else:
                    zero = jnp.zeros((size_x + 8, 8, 2 * LANES), F32)
                    put(target, slice(0, 8 + size_x), rows, zero)

            pl.when(par_y == 1 - side)(functools.partial(fill, 0))
            pl.when(par_y == side)(functools.partial(fill, 1))


def gather_ring(shape, count, fields, near, far, strips, near_strips, corners):
    args = [*fields, near, far, *strips, *near_strips, *corners]
    return pl.pallas_call(
        functools.partial(gather_ring_kernel, count),
        out_shape=[ring_struct(shape)] * 3,
        in_specs=[VMEM] * len(args),
        out_specs=[VMEM] * 3,
        compiler_params=params(),
        cost_estimate=cost(10_000, 4_000_000),
        name="gather_ring",
    )(*args)


def receive_kernel(rounds, cells, p1, p2, q1, q2, *refs):
    size_x, size_y, size_z = p2.shape
    if rounds == 0:
        observed, refs = refs[0], refs[1:]
        refs[2][...] = observed[...]
        synth, born = refs[:2]
    elif rounds > 0:
        earlier, observed = refs[: 2 * rounds], refs[2 * rounds]
        synth, born, spread = refs[2 * rounds + 1 :]
    else:
        synth, born = refs
    steps = synth.shape[0]
    rows, count = size_x * size_y, cells.shape[1]
    flat = cells[...]
    shift = size_z.bit_length() - 1
    row_of = lax.shift_right_logical(flat, shift)
    depth_of = flat - lax.shift_left(row_of, shift)
    pick = lax.broadcasted_iota(jnp.int32, (rows, count), 0) == row_of
    pick = pick.astype(F32).astype(jnp.bfloat16)
    depth = lax.broadcasted_iota(jnp.int32, (LANES, count), 0)
    hits = [depth == depth_of, depth + LANES == depth_of]

    def at(parts):
        total = jnp.zeros((1, count), F32)
        for part, hit in zip(parts, hits):
            rest = part
            picked = None
            for _ in range(3):
                piece = rest.astype(jnp.bfloat16)
                rest = rest - piece.astype(F32)
                got = lax.dot_general(
                    piece, pick, (((0,), (0,)), ((), ())), preferred_element_type=F32
                )
                picked = got if picked is None else picked + got
            total = total + jnp.sum(jnp.where(hit, picked, 0.0), axis=0, keepdims=True)
        return total

    for one, two, target in ((p1, p2, synth), (q1, q2, born)):
        first = [
            one[4 : 4 + size_x, half, 8 : 8 + size_y, :].reshape(rows, LANES) for half in range(2)
        ]
        target[steps - 2 : steps - 1, :] = at(first)
        second = [part.reshape(rows, LANES) for part in halves(two[...])]
        target[steps - 1 : steps, :] = at(second)


    if rounds > 0:
        for k in range(rounds):
            synth[2 * k : 2 * k + 2, :] = earlier[2 * k][...]
            born[2 * k : 2 * k + 2, :] = earlier[2 * k + 1][...]
        residual = observed[...] - synth[...]
        tangent = born[...]
        synth[...] = residual
        numer, denom = jnp.sum(residual * tangent), jnp.sum(tangent * tangent)
        lane = lax.broadcasted_iota(jnp.int32, spread.shape, 2)
        spread[...] = jnp.where(lane == 0, numer, jnp.where(lane == 1, denom, 0.0))


def receive(cells, p1, p2, q1, q2, earlier=(), observed=None, total=0):
    count = cells.shape[1]
    rounds = len(earlier) // 2 if total else (-1 if observed is None else 0)
    outs = [struct(2 * max(rounds, 0) + 2, count)] * 2
    args = [cells, p1, p2, q1, q2]
    if rounds == 0:
        outs.append(struct(*observed.shape))
        args.append(observed)
    elif rounds > 0:
        outs.append(struct(total, 1, LANES))
        args += [*earlier, observed]
    return pl.pallas_call(
        functools.partial(receive_kernel, rounds),
        out_shape=outs,
        in_specs=[VMEM] * len(args),
        out_specs=[VMEM] * len(outs),
        compiler_params=params(),
        cost_estimate=cost(20_000_000, 2_500_000),
        name="receive",
    )(*args)


def finish_kernel(sums, residual, born, speed, smooth, predicted, model, traces, field, sems):
    lane = lax.broadcasted_iota(jnp.int32, sums.shape, 2)
    values = sums[...]
    numer = jnp.sum(jnp.where(lane == 0, values, 0.0))
    denom = jnp.sum(jnp.where(lane == 1, values, 0.0))
    length = jnp.full((1, LANES), numer) / (jnp.full((1, LANES), denom) + 1e-6)
    traces[...] = residual[...] - length * born[...]
    first = pltpu.make_async_copy(traces, predicted, sems.at[0])
    first.start()
    both = jnp.concatenate([length, length], axis=1)
    field[...] = speed[...] + both[None] * smooth[...]
    second = pltpu.make_async_copy(field, model, sems.at[1])
    second.start()
    first.wait()
    second.wait()


def finish(sums, residual, born, speed, smooth):
    outs = [struct(*born.shape), struct(*speed.shape)]
    return pl.pallas_call(
        finish_kernel,
        out_shape=outs,
        in_specs=[VMEM] * 5,
        out_specs=[pl.BlockSpec(memory_space=pl.ANY)] * 2,
        scratch_shapes=[
            pltpu.VMEM(born.shape, F32),
            pltpu.VMEM(speed.shape, F32),
            pltpu.SemaphoreType.DMA((2,)),
        ],
        compiler_params=params(),
        cost_estimate=cost(200_000, 800_000),
        name="finish",
    )(sums, residual, born, speed, smooth)


def smooth_kernel(perturb, p_in, q_in, smooth, p_out, q_out, sems):
    copies = [
        pltpu.make_async_copy(p_in, p_out, sems.at[0]),
        pltpu.make_async_copy(q_in, q_out, sems.at[1]),
    ]
    for copy in copies:
        copy.start()
    size_x, size_y, _ = smooth.shape
    lane = lax.broadcasted_iota(jnp.int32, (size_y, LANES), 1)

    def layer_step(layer, carry):
        parts = []
        for half in range(2):

            def along_x(start, half=half):
                span = slice(start, start + size_y)
                return (
                    0.25 * perturb[layer + 3, half, span, :]
                    + 0.5 * perturb[layer + 4, half, span, :]
                    + 0.25 * perturb[layer + 5, half, span, :]
                )

            parts.append(0.25 * along_x(7) + 0.5 * along_x(8) + 0.25 * along_x(9))
        up = [pltpu.roll(value, LANES - 1, 1) for value in parts]
        down = [pltpu.roll(value, 1, 1) for value in parts]
        keep_up, keep_down = lane < LANES - 1, lane >= 1
        above = [jnp.where(keep_up, up[0], up[1]), jnp.where(keep_up, up[1], 0.0)]
        below = [jnp.where(keep_down, down[0], 0.0), jnp.where(keep_down, down[1], down[0])]
        for half in range(2):
            value = 0.25 * below[half] + 0.5 * parts[half] + 0.25 * above[half]
            smooth[layer, :, half * LANES : (half + 1) * LANES] = value
        return carry

    lax.fori_loop(0, size_x, layer_step, 0)
    for copy in copies:
        copy.wait()


def smoothed(shape, perturb, p_now, q_now):
    return pl.pallas_call(
        smooth_kernel,
        out_shape=[struct(*shape)] * 3,
        in_specs=[VMEM] * 3,
        out_specs=[VMEM] + [pl.BlockSpec(memory_space=pl.ANY)] * 2,
        scratch_shapes=[pltpu.SemaphoreType.DMA((2,))],
        compiler_params=params(),
        cost_estimate=cost(1_000_000, 2_200_000),
        name="smooth",
    )(perturb, p_now, q_now)


def on_device(
    pressure_prev, pressure_now, courant, perturbation, source_pos, wavelet, rec_cells, observed
):
    shape = pressure_now.shape
    size_x, size_y, size_z = shape
    count_x, count_y = lax.axis_size("gx"), lax.axis_size("gy")
    steps = wavelet.shape[0]
    near_x, far_x = near_pairs(count_x), far_pairs(count_x)
    pairs_y = [near_pairs(count_y)]
    if count_y > 2:
        pairs_y.append(far_pairs(count_y))
    count = len(pairs_y)
    far_diagonal = [diagonal(far_x, pairs, count_y) for pairs in pairs_y]

    def swap_near(value):
        return lax.ppermute(value, "gx", near_x)

    def swap_far(value):
        return lax.ppermute(value, "gx", far_x)

    def swap_strips(strips, corners):
        got = [lax.ppermute(value, "gy", pairs) for value, pairs in zip(strips, pairs_y)]
        got_corners = [
            lax.ppermute(value, AXES, pairs) for value, pairs in zip(corners, far_diagonal)
        ]
        return got, [swap_near(value) for value in got], got_corners

    p_far, p_near = swap_far(pressure_now), swap_near(pressure_now)
    far_send, near_send, strips, corners = pack(
        shape, count, pressure_now, pressure_prev, courant, perturbation
    )
    far, near = swap_far(far_send), swap_near(near_send)
    strips, near_strips, corners = swap_strips(strips, corners)
    p_prev, speed, perturb = gather_ring(
        shape,
        count,
        (pressure_prev, courant, perturbation),
        near,
        far,
        strips,
        near_strips,
        corners,
    )
    cells = rec_cells.reshape(1, -1)
    p_cur, q_cur, q_prev = pressure_now, None, None
    q_far = q_near = None
    earlier = []
    traces = observed.reshape(steps, -1)
    for step in range(0, steps, 2):
        around = (strips, near_strips, corners)
        p_pieces = (p_cur, p_near, p_far) + around
        q_pieces = None if q_cur is None else (q_cur, q_near, q_far) + around + (earlier[-1],)
        p_prev, p_cur, drive1, drive2, p_strips = pressure_steps(
            shape, count, step, source_pos, wavelet, p_pieces, p_prev, speed, perturb
        )
        last = step + 2 >= steps
        if not last:
            p_far, p_near = swap_far(p_cur), swap_near(p_cur)
        q_prev, q_cur, strips, corners = tangent_steps(
            shape, count, q_pieces, q_prev, speed, drive1, drive2, p_strips
        )
        if not last:
            strips, near_strips, corners = swap_strips(strips, corners)
            q_far, q_near = swap_far(q_cur), swap_near(q_cur)
        if not last:
            got = list(receive(cells, p_prev, p_cur, q_prev, q_cur, (), traces))
            if step == 0:
                held = got.pop()
            traces = None
            earlier += got
    total = count_x * count_y
    residual, born, spread = receive(
        cells, p_prev, p_cur, q_prev, q_cur, earlier, held, total
    )
    sums = lax.all_to_all(spread, AXES, 0, 0)
    smooth, p_cur, q_cur = smoothed(shape, perturb, p_cur, q_cur)
    predicted, updated_model = finish(sums, residual, born, courant, smooth)
    predicted = predicted.reshape(observed.shape)
    return (p_cur, q_cur, predicted, updated_model)


def solution(mesh):
    field = P("gx", "gy", None)
    traces = P("gx", "gy", None, None)
    return jax.shard_map(
        on_device,
        mesh=mesh,
        in_specs=(field, field, field, field, P(), P(), field, traces),
        out_specs=(field, field, traces, field),
        check_vma=False,
    )
```

```python
import functools

import jax
import jax.numpy as jnp
from jax import lax
from jax.experimental import pallas as pl
from jax.experimental.pallas import tpu as pltpu
from jax.sharding import PartitionSpec as P

COEF = (-205.0 / 72.0, 8.0 / 5.0, -1.0 / 5.0, 8.0 / 315.0, -1.0 / 560.0)
AXES = ("gx", "gy")
LANES = 128
F32 = jnp.float32

VMEM = pl.BlockSpec(memory_space=pltpu.VMEM)


def struct(*shape):
    return jax.ShapeDtypeStruct(shape, F32)


def params():
    return pltpu.CompilerParams(vmem_limit_bytes=24 * 1024 * 1024)


def cost(flops, moved):
    return pl.CostEstimate(flops=flops, bytes_accessed=moved, transcendentals=0)


def near_pairs(count):
    return [(i, i ^ 1) for i in range(count)]


def far_pairs(count):
    pairs = []
    for i in range(1, count - 1, 2):
        pairs += [(i, i + 1), (i + 1, i)]
    return pairs


def diagonal(pairs_x, pairs_y, count_y):
    return [(a * count_y + b, c * count_y + d) for a, c in pairs_x for b, d in pairs_y]


def parity():
    return lax.rem(lax.axis_index("gx"), 2), lax.rem(lax.axis_index("gy"), 2)


def laplace(field, layer, row, rows, lane):
    centre = [field[layer, half, row : row + rows, :] for half in range(2)]
    totals = [(3.0 * COEF[0]) * value for value in centre]
    for k in range(1, 5):
        keep_up = lane < LANES - k
        keep_down = lane >= k
        up = [pltpu.roll(value, LANES - k, 1) for value in centre]
        down = [pltpu.roll(value, k, 1) for value in centre]
        depth = [
            jnp.where(keep_up, up[0], up[1]) + jnp.where(keep_down, down[0], 0.0),
            jnp.where(keep_up, up[1], 0.0) + jnp.where(keep_down, down[1], down[0]),
        ]
        for half in range(2):
            pair = (
                field[layer + k, half, row : row + rows, :]
                + field[layer - k, half, row : row + rows, :]
            )
            pair = pair + (
                field[layer, half, row + k : row + k + rows, :]
                + field[layer, half, row - k : row - k + rows, :]
            )
            totals[half] = totals[half] + COEF[k] * (pair + depth[half])
    return totals


def halves(value):
    return (value[..., :LANES], value[..., LANES:])


def put(target, layers, rows, value):
    for half, part in enumerate(halves(value)):
        target[layers, half, rows, :] = part


def place_wide(wide, scalars, own, near, far, strips, near_strips, corners, first):
    size_x, size_y, _ = own.shape
    par_x = scalars[0]
    par_y = scalars[1]
    inner = slice(16, 16 + size_y)
    put(wide, slice(8, 8 + size_x), inner, own[...])
    near_at = (size_x + 8) * (1 - par_x)
    far_at = (size_x + 8) * par_x
    put(wide, pl.ds(near_at, 8), inner, near[0:8])
    put(wide, pl.ds(far_at, 8), inner, far[0:8])
    for side in range(2):
        rows = slice(8, 16) if side == 0 else slice(16 + size_y, 24 + size_y)

        def fill(which, rows=rows):
            if which < len(strips):
                put(wide, slice(8, 8 + size_x), rows, strips[which][8 * first : 8 * first + 8])
                put(wide, pl.ds(near_at, 8), rows, near_strips[which][8 * first : 8 * first + 8])
                corner_at = 4 + (size_x + 4) * par_x
                put(wide, pl.ds(corner_at, 4), rows, corners[which][4 * first : 4 * first + 4])
            else:
                zero = jnp.zeros((size_x + 8, 8, 2 * LANES), F32)
                put(wide, slice(4, 12 + size_x), rows, zero)

        pl.when(par_y == 1 - side)(functools.partial(fill, 0))
        pl.when(par_y == side)(functools.partial(fill, 1))


def each_side(scalars, count, size_y, present, absent):
    par_y = scalars[1]
    for side in range(2):
        start = 0 if side == 0 else 8 + size_y
        for which in range(2):
            action = present if which < count else absent
            at = 1 - side if which == 0 else side
            pl.when(par_y == at)(functools.partial(action, start))


def send_strips(scalars, value, size_x, size_y):
    even = scalars[1] == 0
    low = value[:, 0:8, :]
    high = value[:, size_y - 8 : size_y, :]
    return [jnp.where(even, high, low), jnp.where(even, low, high)]


def step_pair_kernel(count, sends, tangent, blank, at, *refs):
    refs = list(refs)
    scalars = parity()
    if not tangent:
        sems, source, wave = refs.pop(), refs.pop(-2), refs.pop()
        small = [
            pltpu.make_async_copy(refs[0], source, sems.at[0]),
            pltpu.make_async_copy(refs[1], wave, sems.at[1]),
        ]
        for copy in small:
            copy.start()
        refs = refs[2:]
    if tangent and not blank:
        wide, prev = refs[:2]
        refs = refs[2:]
    elif not blank:
        own, near, far = refs[:3]
        refs = refs[3:]
        strips, refs = refs[:count], refs[count:]
        near_strips, refs = refs[:count], refs[count:]
        corners, refs = refs[:count], refs[count:]
        prev = refs.pop(0)
    speed = refs.pop(0)
    if tangent:
        drive1, drive2 = refs[:2]
        refs = refs[2:]
        partner_strips, refs = refs[:sends], refs[sends:]
    else:
        perturb = refs.pop(0)
    next1, next2 = refs[:2]
    refs = refs[2:]
    if not tangent:
        drive1, drive2 = refs[:2]
        refs = refs[2:]
    strip_out, refs = refs[:sends], refs[sends:]
    if tangent:
        corner_out, refs = refs[:sends], refs[sends:]
    size_x, size_y, _ = next2.shape
    par_x = scalars[0]
    inner = slice(8, 8 + size_y)

    def lanes(rows):
        return lax.broadcasted_iota(jnp.int32, (rows, LANES), 1)

    if not blank:
        if not tangent:
            wide = refs.pop(0)
            place_wide(wide, scalars, own, near, far, strips, near_strips, corners, 0)

        def advance(layer, start, rows):
            laps = laplace(wide, layer + 4, start + 8, rows, lanes(rows))
            span = slice(start, start + rows)
            for half in range(2):
                value = wide[layer + 4, half, start + 8 : start + 8 + rows, :]
                fresh = (
                    2.0 * value
                    - prev[layer, half, span, :]
                    + speed[layer, half, span, :] * laps[half]
                )
                if tangent:
                    fresh = fresh + drive1[layer, half, span, :]
                else:
                    drive1[layer, half, span, :] = perturb[layer, half, span, :] * laps[half]
                next1[layer, half, span, :] = fresh

        for layer in range(size_x + 8):
            advance(layer, 8, size_y)

        def present(start):
            for layer in range(4, 4 + size_x):
                advance(layer, start, 8)

        def absent(start):
            zero = jnp.zeros((size_x, 2, 8, LANES), F32)
            next1[4 : 4 + size_x, :, start : start + 8, :] = zero
            if not tangent:
                drive1[4 : 4 + size_x, :, start : start + 8, :] = zero

        each_side(scalars, count, size_y, present, absent)
    else:
        next1[...] = drive1[...]

    if not tangent:
        for copy in small:
            copy.wait()
        src_x = source[0] - lax.axis_index("gx") * size_x
        src_y = source[1] - lax.axis_index("gy") * size_y
        src_z = source[2]

        @pl.when((src_x >= -4) & (src_x < size_x + 4) & (src_y >= -8) & (src_y < size_y + 8))
        def _():
            half = lax.shift_right_logical(src_z, 7)
            hit = lax.broadcasted_iota(jnp.int32, (1, LANES), 1) == src_z - half * LANES
            row = next1[src_x + 4, half, pl.ds(src_y + 8, 1), :]
            next1[src_x + 4, half, pl.ds(src_y + 8, 1), :] = row + jnp.where(hit, wave[at], 0.0)

    for layer in range(size_x):
        laps = laplace(next1, layer + 4, 8, size_y, lanes(size_y))
        for half in range(2):
            fresh = 2.0 * next1[layer + 4, half, inner, :]
            if not blank:
                fresh = fresh - wide[layer + 8, half, 16 : 16 + size_y, :]
            fresh = fresh + speed[layer + 4, half, inner, :] * laps[half]
            if tangent:
                fresh = fresh + drive2[layer, half]
            else:
                drive2[layer, half] = perturb[layer + 4, half, inner, :] * laps[half]
            next2[layer, :, half * LANES : (half + 1) * LANES] = fresh

    if not tangent:

        @pl.when((src_x >= 0) & (src_x < size_x) & (src_y >= 0) & (src_y < size_y))
        def _():
            hit = lax.broadcasted_iota(jnp.int32, (1, 2 * LANES), 1) == src_z
            row = next2[src_x, pl.ds(src_y, 1), :]
            next2[src_x, pl.ds(src_y, 1), :] = row + jnp.where(hit, wave[at + 1], 0.0)

    made = send_strips(scalars, next2[...], size_x, size_y) if sends else []
    for which in range(sends):
        if not tangent:
            strip_out[which][...] = made[which]
        else:
            strip_out[which][0:size_x] = partner_strips[which][...]
            strip_out[which][size_x : 2 * size_x] = made[which]
            facing = pl.ds((size_x - 4) * par_x, 4)
            corner_out[which][0:4] = partner_strips[which][facing]
            strip = strip_out[which][pl.ds(size_x + (size_x - 4) * par_x, 4)]
            corner_out[which][4:8] = strip


def place_kernel(count, own, near, far, *refs):
    strips, near_strips, corners = (refs[k * count : (k + 1) * count] for k in range(3))
    place_wide(refs[-1], parity(), own, near, far, strips, near_strips, corners, 1)


def wide_shape(shape):
    return pltpu.VMEM((shape[0] + 16, 2, shape[1] + 32, LANES), F32)


def ring_struct(shape):
    return struct(shape[0] + 8, 2, shape[1] + 16, LANES)


def pressure_steps(shape, count, sends, at, source, wave, pieces, prev, speed, perturb):
    own, near, far, strips, near_strips, corners = pieces
    outs = [ring_struct(shape), struct(*shape), ring_struct(shape)]
    outs += [struct(shape[0], 2, shape[1], LANES)]
    outs += [struct(shape[0], 8, shape[2])] * sends
    args = [own, near, far, *strips, *near_strips, *corners, prev, speed, perturb]
    out = pl.pallas_call(
        functools.partial(step_pair_kernel, count, sends, False, False, at),
        out_shape=outs,
        in_specs=[pl.BlockSpec(memory_space=pl.ANY)] * 2 + [VMEM] * len(args),
        out_specs=[VMEM] * len(outs),
        scratch_shapes=[
            wide_shape(shape),
            pltpu.SMEM(source.shape, jnp.int32),
            pltpu.SMEM(wave.shape, F32),
            pltpu.SemaphoreType.DMA((2,)),
        ],
        compiler_params=params(),
        cost_estimate=cost(900_000_000, 400_000_000),
        name="pressure_steps",
    )(source, wave, *args)
    return out[0], out[1], out[2], out[3], list(out[4:])


def tangent_steps(shape, count, sends, pieces, prev, speed, drive1, drive2, partner_strips):
    blank = pieces is None
    outs = [ring_struct(shape), struct(*shape)]
    outs += [struct(2 * shape[0], 8, shape[2])] * sends
    outs += [struct(8, 8, shape[2])] * sends
    args = []
    if not blank:
        own, near, far, strips, near_strips, corners, done = pieces
        args = [own, near, far, *strips, *near_strips, *corners, done]
        wide = pl.pallas_call(
            functools.partial(place_kernel, count),
            out_shape=struct(shape[0] + 16, 2, shape[1] + 32, LANES),
            in_specs=[VMEM] * len(args),
            out_specs=VMEM,
            compiler_params=params(),
            cost_estimate=cost(10_000, 3_000_000),
            name="place",
        )(*args)
        args = [wide, prev]
    args += [speed, drive1, drive2, *partner_strips]
    out = pl.pallas_call(
        functools.partial(step_pair_kernel, count, sends, True, blank, 0),
        out_shape=outs,
        in_specs=[VMEM] * len(args),
        out_specs=[VMEM] * len(outs),
        compiler_params=params(),
        cost_estimate=cost(900_000_000, 400_000_000),
        name="tangent_steps",
    )(*args)
    return out[0], out[1], list(out[2 : 2 + sends]), list(out[2 + sends :])


def pack_kernel(count, p_now, p_prev, speed, perturb, far, near, *rest):
    size_x, size_y, _ = p_now.shape
    strips, corners, sems = rest[:count], rest[count : 2 * count], rest[2 * count]
    par_x, par_y = parity()
    far_face = pl.ds((size_x - 4) * par_x, 4)
    near_face = pl.ds((size_x - 4) * (1 - par_x), 4)
    moves = []
    for target, face in ((far, far_face), (near, near_face)):
        for k, field in enumerate((p_prev, speed, perturb)):
            start = 4 * k
            moves.append((field.at[face], target.at[start : start + 4]))
    for which in range(count):
        high = 1 - par_y if which == 0 else par_y
        rows = pl.ds(pl.multiple_of(high * (size_y - 8), 8), 8)
        for k, field in enumerate((p_now, perturb, p_prev, speed)):
            moves.append((field.at[:, rows], strips[which].at[k * size_x : (k + 1) * size_x]))
            if k < 2:
                moves.append((field.at[far_face, rows], corners[which].at[4 * k : 4 * k + 4]))
    copies = [
        pltpu.make_async_copy(source, target, sems.at[k]) for k, (source, target) in enumerate(moves)
    ]
    for copy in copies:
        copy.start()
    for copy in copies:
        copy.wait()


def pack(shape, count, p_now, p_prev, speed, perturb):
    outs = [struct(12, shape[1], shape[2])] * 2
    outs += [struct(4 * shape[0], 8, shape[2])] * count
    outs += [struct(8, 8, shape[2])] * count
    out = pl.pallas_call(
        functools.partial(pack_kernel, count),
        out_shape=outs,
        in_specs=[pl.BlockSpec(memory_space=pl.ANY)] * 4,
        out_specs=[VMEM] * len(outs),
        scratch_shapes=[pltpu.SemaphoreType.DMA((6 + 6 * count,))],
        compiler_params=pltpu.CompilerParams(vmem_limit_bytes=58 * 1024 * 1024),
        cost_estimate=cost(10_000, 3_000_000),
        name="pack",
    )(p_now, p_prev, speed, perturb)
    return out[0], out[1], list(out[2 : 2 + count]), list(out[2 + count :])


def gather_ring_kernel(count, p_prev, speed, perturb, near, far, *refs):
    strips, refs = refs[:count], refs[count:]
    near_strips, refs = refs[:count], refs[count:]
    corners, targets = refs[:count], refs[count:]
    size_x, size_y, _ = p_prev.shape
    par_x, par_y = parity()
    inner = slice(8, 8 + size_y)
    near_at = (size_x + 4) * (1 - par_x)
    far_at = (size_x + 4) * par_x
    for k, (own, target) in enumerate(zip((p_prev, speed, perturb), targets)):
        put(target, slice(4, 4 + size_x), inner, own[...])
        face = slice(4 * k, 4 * k + 4)
        put(target, pl.ds(near_at, 4), inner, near[face])
        put(target, pl.ds(far_at, 4), inner, far[face])
        part = (2, 3, 1)[k]
        for side in range(2):
            rows = slice(0, 8) if side == 0 else slice(8 + size_y, 16 + size_y)

            def fill(which, k=k, rows=rows, target=target, part=part):
                if which < count:
                    base = part * size_x
                    put(target, slice(4, 4 + size_x), rows, strips[which][base : base + size_x])
                    if k == 2:
                        face = pl.ds(base + (size_x - 4) * par_x, 4)
                        put(target, pl.ds(near_at, 4), rows, near_strips[which][face])
                        put(target, pl.ds(far_at, 4), rows, corners[which][4:8])
                else:
                    zero = jnp.zeros((size_x + 8, 8, 2 * LANES), F32)
                    put(target, slice(0, 8 + size_x), rows, zero)

            pl.when(par_y == 1 - side)(functools.partial(fill, 0))
            pl.when(par_y == side)(functools.partial(fill, 1))


def gather_ring(shape, count, fields, near, far, strips, near_strips, corners):
    args = [*fields, near, far, *strips, *near_strips, *corners]
    return pl.pallas_call(
        functools.partial(gather_ring_kernel, count),
        out_shape=[ring_struct(shape)] * 3,
        in_specs=[VMEM] * len(args),
        out_specs=[VMEM] * 3,
        compiler_params=params(),
        cost_estimate=cost(10_000, 4_000_000),
        name="gather_ring",
    )(*args)


def receive_kernel(rounds, cells, p1, p2, q1, q2, *refs):
    size_x, size_y, size_z = p2.shape
    if rounds == 0:
        observed, refs = refs[0], refs[1:]
        refs[2][...] = observed[...]
        synth, born = refs[:2]
    elif rounds > 0:
        earlier, observed = refs[: 2 * rounds], refs[2 * rounds]
        synth, born, spread = refs[2 * rounds + 1 :]
    else:
        synth, born = refs
    steps = synth.shape[0]
    rows, count = size_x * size_y, cells.shape[1]
    flat = cells[...]
    shift = size_z.bit_length() - 1
    row_of = lax.shift_right_logical(flat, shift)
    depth_of = flat - lax.shift_left(row_of, shift)
    pick = lax.broadcasted_iota(jnp.int32, (rows, count), 0) == row_of
    pick = pick.astype(F32).astype(jnp.bfloat16)
    depth = lax.broadcasted_iota(jnp.int32, (LANES, count), 0)
    hits = [depth == depth_of, depth + LANES == depth_of]

    def at(parts):
        total = jnp.zeros((1, count), F32)
        for part, hit in zip(parts, hits):
            rest = part
            picked = None
            for _ in range(3):
                piece = rest.astype(jnp.bfloat16)
                rest = rest - piece.astype(F32)
                got = lax.dot_general(
                    piece, pick, (((0,), (0,)), ((), ())), preferred_element_type=F32
                )
                picked = got if picked is None else picked + got
            total = total + jnp.sum(jnp.where(hit, picked, 0.0), axis=0, keepdims=True)
        return total

    for one, two, target in ((p1, p2, synth), (q1, q2, born)):
        first = [
            one[4 : 4 + size_x, half, 8 : 8 + size_y, :].reshape(rows, LANES) for half in range(2)
        ]
        target[steps - 2 : steps - 1, :] = at(first)
        second = [part.reshape(rows, LANES) for part in halves(two[...])]
        target[steps - 1 : steps, :] = at(second)


    if rounds > 0:
        for k in range(rounds):
            synth[2 * k : 2 * k + 2, :] = earlier[2 * k][...]
            born[2 * k : 2 * k + 2, :] = earlier[2 * k + 1][...]
        residual = observed[...] - synth[...]
        tangent = born[...]
        synth[...] = residual
        numer, denom = jnp.sum(residual * tangent), jnp.sum(tangent * tangent)
        lane = lax.broadcasted_iota(jnp.int32, spread.shape, 2)
        spread[...] = jnp.where(lane == 0, numer, jnp.where(lane == 1, denom, 0.0))


def receive(cells, p1, p2, q1, q2, earlier=(), observed=None, total=0):
    count = cells.shape[1]
    rounds = len(earlier) // 2 if total else (-1 if observed is None else 0)
    outs = [struct(2 * max(rounds, 0) + 2, count)] * 2
    args = [cells, p1, p2, q1, q2]
    if rounds == 0:
        outs.append(struct(*observed.shape))
        args.append(observed)
    elif rounds > 0:
        outs.append(struct(total, 1, LANES))
        args += [*earlier, observed]
    return pl.pallas_call(
        functools.partial(receive_kernel, rounds),
        out_shape=outs,
        in_specs=[VMEM] * len(args),
        out_specs=[VMEM] * len(outs),
        compiler_params=params(),
        cost_estimate=cost(20_000_000, 2_500_000),
        name="receive",
    )(*args)


def finish_kernel(sums, residual, born, speed, smooth, predicted, model, traces, field, sems):
    lane = lax.broadcasted_iota(jnp.int32, sums.shape, 2)
    values = sums[...]
    numer = jnp.sum(jnp.where(lane == 0, values, 0.0))
    denom = jnp.sum(jnp.where(lane == 1, values, 0.0))
    length = jnp.full((1, LANES), numer) / (jnp.full((1, LANES), denom) + 1e-6)
    traces[...] = residual[...] - length * born[...]
    first = pltpu.make_async_copy(traces, predicted, sems.at[0])
    first.start()
    both = jnp.concatenate([length, length], axis=1)
    field[...] = speed[...] + both[None] * smooth[...]
    second = pltpu.make_async_copy(field, model, sems.at[1])
    second.start()
    first.wait()
    second.wait()


def finish(sums, residual, born, speed, smooth):
    outs = [struct(*born.shape), struct(*speed.shape)]
    return pl.pallas_call(
        finish_kernel,
        out_shape=outs,
        in_specs=[VMEM] * 5,
        out_specs=[pl.BlockSpec(memory_space=pl.ANY)] * 2,
        scratch_shapes=[
            pltpu.VMEM(born.shape, F32),
            pltpu.VMEM(speed.shape, F32),
            pltpu.SemaphoreType.DMA((2,)),
        ],
        compiler_params=params(),
        cost_estimate=cost(200_000, 800_000),
        name="finish",
    )(sums, residual, born, speed, smooth)


def smooth_kernel(perturb, p_in, q_in, smooth, p_out, q_out, sems):
    copies = [
        pltpu.make_async_copy(p_in, p_out, sems.at[0]),
        pltpu.make_async_copy(q_in, q_out, sems.at[1]),
    ]
    for copy in copies:
        copy.start()
    size_x, size_y, _ = smooth.shape
    lane = lax.broadcasted_iota(jnp.int32, (size_y, LANES), 1)

    def layer_step(layer, carry):
        parts = []
        for half in range(2):

            def along_x(start, half=half):
                span = slice(start, start + size_y)
                return (
                    0.25 * perturb[layer + 3, half, span, :]
                    + 0.5 * perturb[layer + 4, half, span, :]
                    + 0.25 * perturb[layer + 5, half, span, :]
                )

            parts.append(0.25 * along_x(7) + 0.5 * along_x(8) + 0.25 * along_x(9))
        up = [pltpu.roll(value, LANES - 1, 1) for value in parts]
        down = [pltpu.roll(value, 1, 1) for value in parts]
        keep_up, keep_down = lane < LANES - 1, lane >= 1
        above = [jnp.where(keep_up, up[0], up[1]), jnp.where(keep_up, up[1], 0.0)]
        below = [jnp.where(keep_down, down[0], 0.0), jnp.where(keep_down, down[1], down[0])]
        for half in range(2):
            value = 0.25 * below[half] + 0.5 * parts[half] + 0.25 * above[half]
            smooth[layer, :, half * LANES : (half + 1) * LANES] = value
        return carry

    lax.fori_loop(0, size_x, layer_step, 0)
    for copy in copies:
        copy.wait()


def smoothed(shape, perturb, p_now, q_now):
    return pl.pallas_call(
        smooth_kernel,
        out_shape=[struct(*shape)] * 3,
        in_specs=[VMEM] * 3,
        out_specs=[VMEM] + [pl.BlockSpec(memory_space=pl.ANY)] * 2,
        scratch_shapes=[pltpu.SemaphoreType.DMA((2,))],
        compiler_params=params(),
        cost_estimate=cost(1_000_000, 2_200_000),
        name="smooth",
    )(perturb, p_now, q_now)


def on_device(
    pressure_prev, pressure_now, courant, perturbation, source_pos, wavelet, rec_cells, observed
):
    shape = pressure_now.shape
    size_x, size_y, size_z = shape
    count_x, count_y = lax.axis_size("gx"), lax.axis_size("gy")
    steps = wavelet.shape[0]
    near_x, far_x = near_pairs(count_x), far_pairs(count_x)
    pairs_y = [near_pairs(count_y)]
    if count_y > 2:
        pairs_y.append(far_pairs(count_y))
    count = len(pairs_y)
    far_diagonal = [diagonal(far_x, pairs, count_y) for pairs in pairs_y]

    def swap_near(value):
        return lax.ppermute(value, "gx", near_x)

    def swap_far(value):
        return lax.ppermute(value, "gx", far_x)

    def swap_strips(strips, corners):
        got = [lax.ppermute(value, "gy", pairs) for value, pairs in zip(strips, pairs_y)]
        got_corners = [
            lax.ppermute(value, AXES, pairs) for value, pairs in zip(corners, far_diagonal)
        ]
        return got, [swap_near(value) for value in got], got_corners

    p_far, p_near = swap_far(pressure_now), swap_near(pressure_now)
    far_send, near_send, strips, corners = pack(
        shape, count, pressure_now, pressure_prev, courant, perturbation
    )
    far, near = swap_far(far_send), swap_near(near_send)
    strips, near_strips, corners = swap_strips(strips, corners)
    p_prev, speed, perturb = gather_ring(
        shape,
        count,
        (pressure_prev, courant, perturbation),
        near,
        far,
        strips,
        near_strips,
        corners,
    )
    cells = rec_cells.reshape(1, -1)
    p_cur, q_cur, q_prev = pressure_now, None, None
    q_far = q_near = None
    earlier = []
    traces = observed.reshape(steps, -1)
    for step in range(0, steps, 2):
        last = step + 2 >= steps
        sends = 0 if last else count
        around = (strips, near_strips, corners)
        p_pieces = (p_cur, p_near, p_far) + around
        q_pieces = None if q_cur is None else (q_cur, q_near, q_far) + around + (earlier[-1],)
        p_prev, p_cur, drive1, drive2, p_strips = pressure_steps(
            shape, count, sends, step, source_pos, wavelet, p_pieces, p_prev, speed, perturb
        )
        if not last:
            p_far, p_near = swap_far(p_cur), swap_near(p_cur)
        q_prev, q_cur, strips, corners = tangent_steps(
            shape, count, sends, q_pieces, q_prev, speed, drive1, drive2, p_strips
        )
        if not last:
            strips, near_strips, corners = swap_strips(strips, corners)
            q_far, q_near = swap_far(q_cur), swap_near(q_cur)
        if not last:
            got = list(receive(cells, p_prev, p_cur, q_prev, q_cur, (), traces))
            if step == 0:
                held = got.pop()
            traces = None
            earlier += got
    total = count_x * count_y
    residual, born, spread = receive(
        cells, p_prev, p_cur, q_prev, q_cur, earlier, held, total
    )
    sums = lax.all_to_all(spread, AXES, 0, 0)
    smooth, p_cur, q_cur = smoothed(shape, perturb, p_cur, q_cur)
    predicted, updated_model = finish(sums, residual, born, courant, smooth)
    predicted = predicted.reshape(observed.shape)
    return (p_cur, q_cur, predicted, updated_model)


def solution(mesh):
    field = P("gx", "gy", None)
    traces = P("gx", "gy", None, None)
    return jax.shard_map(
        on_device,
        mesh=mesh,
        in_specs=(field, field, field, field, P(), P(), field, traces),
        out_specs=(field, field, traces, field),
        check_vma=False,
    )
```

```python
import functools

import jax
import jax.numpy as jnp
from jax import lax
from jax.experimental import pallas as pl
from jax.experimental.pallas import tpu as pltpu
from jax.sharding import PartitionSpec as P

COEF = (-205.0 / 72.0, 8.0 / 5.0, -1.0 / 5.0, 8.0 / 315.0, -1.0 / 560.0)
AXES = ("gx", "gy")
LANES = 128
F32 = jnp.float32

VMEM = pl.BlockSpec(memory_space=pltpu.VMEM)


def struct(*shape):
    return jax.ShapeDtypeStruct(shape, F32)


def params():
    return pltpu.CompilerParams(vmem_limit_bytes=24 * 1024 * 1024)


def cost(flops, moved):
    return pl.CostEstimate(flops=flops, bytes_accessed=moved, transcendentals=0)


def near_pairs(count):
    return [(i, i ^ 1) for i in range(count)]


def far_pairs(count):
    pairs = []
    for i in range(1, count - 1, 2):
        pairs += [(i, i + 1), (i + 1, i)]
    return pairs


def diagonal(pairs_x, pairs_y, count_y):
    return [(a * count_y + b, c * count_y + d) for a, c in pairs_x for b, d in pairs_y]


def parity():
    return lax.rem(lax.axis_index("gx"), 2), lax.rem(lax.axis_index("gy"), 2)


def laplace(field, layer, row, rows, lane):
    centre = [field[layer, half, row : row + rows, :] for half in range(2)]
    totals = [(3.0 * COEF[0]) * value for value in centre]
    for k in range(1, 5):
        keep_up = lane < LANES - k
        keep_down = lane >= k
        up = [pltpu.roll(value, LANES - k, 1) for value in centre]
        down = [pltpu.roll(value, k, 1) for value in centre]
        depth = [
            jnp.where(keep_up, up[0], up[1]) + jnp.where(keep_down, down[0], 0.0),
            jnp.where(keep_up, up[1], 0.0) + jnp.where(keep_down, down[1], down[0]),
        ]
        for half in range(2):
            pair = (
                field[layer + k, half, row : row + rows, :]
                + field[layer - k, half, row : row + rows, :]
            )
            pair = pair + (
                field[layer, half, row + k : row + k + rows, :]
                + field[layer, half, row - k : row - k + rows, :]
            )
            totals[half] = totals[half] + COEF[k] * (pair + depth[half])
    return totals


def halves(value):
    return (value[..., :LANES], value[..., LANES:])


def put(target, layers, rows, value):
    for half, part in enumerate(halves(value)):
        target[layers, half, rows, :] = part


def place_wide(wide, scalars, own, near, far, strips, near_strips, corners, first):
    size_x, size_y, _ = own.shape
    par_x = scalars[0]
    par_y = scalars[1]
    inner = slice(16, 16 + size_y)
    put(wide, slice(8, 8 + size_x), inner, own[...])
    near_at = (size_x + 8) * (1 - par_x)
    far_at = (size_x + 8) * par_x
    put(wide, pl.ds(near_at, 8), inner, near[0:8])
    put(wide, pl.ds(far_at, 8), inner, far[0:8])
    for side in range(2):
        rows = slice(8, 16) if side == 0 else slice(16 + size_y, 24 + size_y)

        def fill(which, rows=rows):
            if which < len(strips):
                put(wide, slice(8, 8 + size_x), rows, strips[which][8 * first : 8 * first + 8])
                put(wide, pl.ds(near_at, 8), rows, near_strips[which][8 * first : 8 * first + 8])
                corner_at = 4 + (size_x + 4) * par_x
                put(wide, pl.ds(corner_at, 4), rows, corners[which][4 * first : 4 * first + 4])
            else:
                zero = jnp.zeros((size_x + 8, 8, 2 * LANES), F32)
                put(wide, slice(4, 12 + size_x), rows, zero)

        pl.when(par_y == 1 - side)(functools.partial(fill, 0))
        pl.when(par_y == side)(functools.partial(fill, 1))


def each_side(scalars, count, size_y, present, absent):
    par_y = scalars[1]
    for side in range(2):
        start = 0 if side == 0 else 8 + size_y
        for which in range(2):
            action = present if which < count else absent
            at = 1 - side if which == 0 else side
            pl.when(par_y == at)(functools.partial(action, start))


def send_strips(scalars, value, size_x, size_y):
    even = scalars[1] == 0
    low = value[:, 0:8, :]
    high = value[:, size_y - 8 : size_y, :]
    return [jnp.where(even, high, low), jnp.where(even, low, high)]


def step_pair_kernel(count, sends, tangent, blank, at, *refs):
    refs = list(refs)
    scalars = parity()
    if not tangent:
        sems, source, wave = refs.pop(), refs.pop(-2), refs.pop()
        small = [
            pltpu.make_async_copy(refs[0], source, sems.at[0]),
            pltpu.make_async_copy(refs[1], wave, sems.at[1]),
        ]
        for copy in small:
            copy.start()
        refs = refs[2:]
    if tangent and not blank:
        wide, prev = refs[:2]
        refs = refs[2:]
    elif not blank:
        own, near, far = refs[:3]
        refs = refs[3:]
        strips, refs = refs[:count], refs[count:]
        near_strips, refs = refs[:count], refs[count:]
        corners, refs = refs[:count], refs[count:]
        prev = refs.pop(0)
    speed = refs.pop(0)
    if tangent:
        drive1, drive2 = refs[:2]
        refs = refs[2:]
        partner_strips, refs = refs[:sends], refs[sends:]
    else:
        perturb = refs.pop(0)
    next1, next2 = refs[:2]
    refs = refs[2:]
    if not tangent:
        drive1, drive2 = refs[:2]
        refs = refs[2:]
    strip_out, refs = refs[:sends], refs[sends:]
    if tangent:
        corner_out, refs = refs[:sends], refs[sends:]
    size_x, size_y, _ = next2.shape
    par_x = scalars[0]
    inner = slice(8, 8 + size_y)

    def lanes(rows):
        return lax.broadcasted_iota(jnp.int32, (rows, LANES), 1)

    if not blank:
        if not tangent:
            wide = refs.pop(0)
            place_wide(wide, scalars, own, near, far, strips, near_strips, corners, 0)

        def advance(layer, start, rows):
            laps = laplace(wide, layer + 4, start + 8, rows, lanes(rows))
            span = slice(start, start + rows)
            for half in range(2):
                value = wide[layer + 4, half, start + 8 : start + 8 + rows, :]
                fresh = (
                    2.0 * value
                    - prev[layer, half, span, :]
                    + speed[layer, half, span, :] * laps[half]
                )
                if tangent:
                    fresh = fresh + drive1[layer, half, span, :]
                else:
                    drive1[layer, half, span, :] = perturb[layer, half, span, :] * laps[half]
                next1[layer, half, span, :] = fresh

        for layer in range(size_x + 8):
            advance(layer, 8, size_y)

        def present(start):
            for layer in range(4, 4 + size_x):
                advance(layer, start, 8)

        def absent(start):
            zero = jnp.zeros((size_x, 2, 8, LANES), F32)
            next1[4 : 4 + size_x, :, start : start + 8, :] = zero
            if not tangent:
                drive1[4 : 4 + size_x, :, start : start + 8, :] = zero

        each_side(scalars, count, size_y, present, absent)
    else:
        next1[...] = drive1[...]

    if not tangent:
        for copy in small:
            copy.wait()
        src_x = source[0] - lax.axis_index("gx") * size_x
        src_y = source[1] - lax.axis_index("gy") * size_y
        src_z = source[2]

        @pl.when((src_x >= -4) & (src_x < size_x + 4) & (src_y >= -8) & (src_y < size_y + 8))
        def _():
            half = lax.shift_right_logical(src_z, 7)
            hit = lax.broadcasted_iota(jnp.int32, (1, LANES), 1) == src_z - half * LANES
            row = next1[src_x + 4, half, pl.ds(src_y + 8, 1), :]
            next1[src_x + 4, half, pl.ds(src_y + 8, 1), :] = row + jnp.where(hit, wave[at], 0.0)

    for layer in range(size_x):
        laps = laplace(next1, layer + 4, 8, size_y, lanes(size_y))
        for half in range(2):
            fresh = 2.0 * next1[layer + 4, half, inner, :]
            if not blank:
                fresh = fresh - wide[layer + 8, half, 16 : 16 + size_y, :]
            fresh = fresh + speed[layer + 4, half, inner, :] * laps[half]
            if tangent:
                fresh = fresh + drive2[layer, half]
            else:
                drive2[layer, half] = perturb[layer + 4, half, inner, :] * laps[half]
            next2[layer, :, half * LANES : (half + 1) * LANES] = fresh

    if not tangent:

        @pl.when((src_x >= 0) & (src_x < size_x) & (src_y >= 0) & (src_y < size_y))
        def _():
            hit = lax.broadcasted_iota(jnp.int32, (1, 2 * LANES), 1) == src_z
            row = next2[src_x, pl.ds(src_y, 1), :]
            next2[src_x, pl.ds(src_y, 1), :] = row + jnp.where(hit, wave[at + 1], 0.0)

    made = send_strips(scalars, next2[...], size_x, size_y) if sends else []
    for which in range(sends):
        if not tangent:
            strip_out[which][...] = made[which]
        else:
            strip_out[which][0:size_x] = partner_strips[which][...]
            strip_out[which][size_x : 2 * size_x] = made[which]
            facing = pl.ds((size_x - 4) * par_x, 4)
            corner_out[which][0:4] = partner_strips[which][facing]
            strip = strip_out[which][pl.ds(size_x + (size_x - 4) * par_x, 4)]
            corner_out[which][4:8] = strip


def place_kernel(count, own, near, far, *refs):
    strips, near_strips, corners = (refs[k * count : (k + 1) * count] for k in range(3))
    place_wide(refs[-1], parity(), own, near, far, strips, near_strips, corners, 1)


def wide_shape(shape):
    return pltpu.VMEM((shape[0] + 16, 2, shape[1] + 32, LANES), F32)


def ring_struct(shape):
    return struct(shape[0] + 8, 2, shape[1] + 16, LANES)


def pressure_steps(shape, count, sends, at, source, wave, pieces, prev, speed, perturb):
    own, near, far, strips, near_strips, corners = pieces
    outs = [ring_struct(shape), struct(*shape), ring_struct(shape)]
    outs += [struct(shape[0], 2, shape[1], LANES)]
    outs += [struct(shape[0], 8, shape[2])] * sends
    args = [own, near, far, *strips, *near_strips, *corners, prev, speed, perturb]
    out = pl.pallas_call(
        functools.partial(step_pair_kernel, count, sends, False, False, at),
        out_shape=outs,
        in_specs=[pl.BlockSpec(memory_space=pl.ANY)] * 2 + [VMEM] * len(args),
        out_specs=[VMEM] * len(outs),
        scratch_shapes=[
            wide_shape(shape),
            pltpu.SMEM(source.shape, jnp.int32),
            pltpu.SMEM(wave.shape, F32),
            pltpu.SemaphoreType.DMA((2,)),
        ],
        compiler_params=params(),
        cost_estimate=cost(900_000_000, 400_000_000),
        name="pressure_steps",
    )(source, wave, *args)
    return out[0], out[1], out[2], out[3], list(out[4:])


def tangent_steps(shape, count, sends, pieces, prev, speed, drive1, drive2, partner_strips):
    blank = pieces is None
    outs = [ring_struct(shape), struct(*shape)]
    outs += [struct(2 * shape[0], 8, shape[2])] * sends
    outs += [struct(8, 8, shape[2])] * sends
    args = []
    if not blank:
        own, near, far, strips, near_strips, corners, done = pieces
        args = [own, near, far, *strips, *near_strips, *corners, done]
        wide = pl.pallas_call(
            functools.partial(place_kernel, count),
            out_shape=struct(shape[0] + 16, 2, shape[1] + 32, LANES),
            in_specs=[VMEM] * len(args),
            out_specs=VMEM,
            compiler_params=params(),
            cost_estimate=cost(10_000, 3_000_000),
            name="place",
        )(*args)
        args = [wide, prev]
    args += [speed, drive1, drive2, *partner_strips]
    out = pl.pallas_call(
        functools.partial(step_pair_kernel, count, sends, True, blank, 0),
        out_shape=outs,
        in_specs=[VMEM] * len(args),
        out_specs=[VMEM] * len(outs),
        compiler_params=params(),
        cost_estimate=cost(900_000_000, 400_000_000),
        name="tangent_steps",
    )(*args)
    return out[0], out[1], list(out[2 : 2 + sends]), list(out[2 + sends :])


def pack_kernel(count, p_now, p_prev, speed, perturb, far, near, *rest):
    size_x, size_y, _ = p_now.shape
    strips, corners, sems = rest[:count], rest[count : 2 * count], rest[2 * count]
    par_x, par_y = parity()
    far_face = pl.ds((size_x - 4) * par_x, 4)
    near_face = pl.ds((size_x - 4) * (1 - par_x), 4)
    moves = []
    for target, face in ((far, far_face), (near, near_face)):
        for k, field in enumerate((p_prev, speed, perturb)):
            start = 4 * k
            moves.append((field.at[face], target.at[start : start + 4]))
    for which in range(count):
        high = 1 - par_y if which == 0 else par_y
        rows = pl.ds(pl.multiple_of(high * (size_y - 8), 8), 8)
        for k, field in enumerate((p_now, perturb, p_prev, speed)):
            moves.append((field.at[:, rows], strips[which].at[k * size_x : (k + 1) * size_x]))
            if k < 2:
                moves.append((field.at[far_face, rows], corners[which].at[4 * k : 4 * k + 4]))
    copies = [
        pltpu.make_async_copy(source, target, sems.at[k]) for k, (source, target) in enumerate(moves)
    ]
    for copy in copies:
        copy.start()
    for copy in copies:
        copy.wait()


def pack(shape, count, p_now, p_prev, speed, perturb):
    outs = [struct(12, shape[1], shape[2])] * 2
    outs += [struct(4 * shape[0], 8, shape[2])] * count
    outs += [struct(8, 8, shape[2])] * count
    out = pl.pallas_call(
        functools.partial(pack_kernel, count),
        out_shape=outs,
        in_specs=[pl.BlockSpec(memory_space=pl.ANY)] * 4,
        out_specs=[VMEM] * len(outs),
        scratch_shapes=[pltpu.SemaphoreType.DMA((6 + 6 * count,))],
        compiler_params=pltpu.CompilerParams(vmem_limit_bytes=58 * 1024 * 1024),
        cost_estimate=cost(10_000, 3_000_000),
        name="pack",
    )(p_now, p_prev, speed, perturb)
    return out[0], out[1], list(out[2 : 2 + count]), list(out[2 + count :])


def gather_ring_kernel(count, p_prev, speed, perturb, near, far, *refs):
    strips, refs = refs[:count], refs[count:]
    near_strips, refs = refs[:count], refs[count:]
    corners, targets = refs[:count], refs[count:]
    size_x, size_y, _ = p_prev.shape
    par_x, par_y = parity()
    inner = slice(8, 8 + size_y)
    near_at = (size_x + 4) * (1 - par_x)
    far_at = (size_x + 4) * par_x
    for k, (own, target) in enumerate(zip((p_prev, speed, perturb), targets)):
        put(target, slice(4, 4 + size_x), inner, own[...])
        face = slice(4 * k, 4 * k + 4)
        put(target, pl.ds(near_at, 4), inner, near[face])
        put(target, pl.ds(far_at, 4), inner, far[face])
        part = (2, 3, 1)[k]
        for side in range(2):
            rows = slice(0, 8) if side == 0 else slice(8 + size_y, 16 + size_y)

            def fill(which, k=k, rows=rows, target=target, part=part):
                if which < count:
                    base = part * size_x
                    put(target, slice(4, 4 + size_x), rows, strips[which][base : base + size_x])
                    if k == 2:
                        face = pl.ds(base + (size_x - 4) * par_x, 4)
                        put(target, pl.ds(near_at, 4), rows, near_strips[which][face])
                        put(target, pl.ds(far_at, 4), rows, corners[which][4:8])
                else:
                    zero = jnp.zeros((size_x + 8, 8, 2 * LANES), F32)
                    put(target, slice(0, 8 + size_x), rows, zero)

            pl.when(par_y == 1 - side)(functools.partial(fill, 0))
            pl.when(par_y == side)(functools.partial(fill, 1))


def gather_ring(shape, count, fields, near, far, strips, near_strips, corners):
    args = [*fields, near, far, *strips, *near_strips, *corners]
    return pl.pallas_call(
        functools.partial(gather_ring_kernel, count),
        out_shape=[ring_struct(shape)] * 3,
        in_specs=[VMEM] * len(args),
        out_specs=[VMEM] * 3,
        compiler_params=params(),
        cost_estimate=cost(10_000, 4_000_000),
        name="gather_ring",
    )(*args)


def receive_kernel(rounds, cells, p1, p2, q1, q2, *refs):
    size_x, size_y, size_z = q2.shape
    if rounds == 0:
        observed, refs = refs[0], refs[1:]
        refs[2][...] = observed[...]
        synth, born = refs[:2]
    elif rounds > 0:
        earlier, observed = refs[: 2 * rounds], refs[2 * rounds]
        synth, born, spread = refs[2 * rounds + 1 :]
    else:
        synth, born = refs
    steps = synth.shape[0]
    rows, count = size_x * size_y, cells.shape[1]
    flat = cells[...]
    shift = size_z.bit_length() - 1
    row_of = lax.shift_right_logical(flat, shift)
    depth_of = flat - lax.shift_left(row_of, shift)
    pick = lax.broadcasted_iota(jnp.int32, (rows, count), 0) == row_of
    pick = pick.astype(F32).astype(jnp.bfloat16)
    depth = lax.broadcasted_iota(jnp.int32, (LANES, count), 0)
    hits = [depth == depth_of, depth + LANES == depth_of]

    def at(parts):
        total = jnp.zeros((1, count), F32)
        for part, hit in zip(parts, hits):
            rest = part
            picked = None
            for _ in range(3):
                piece = rest.astype(jnp.bfloat16)
                rest = rest - piece.astype(F32)
                got = lax.dot_general(
                    piece, pick, (((0,), (0,)), ((), ())), preferred_element_type=F32
                )
                picked = got if picked is None else picked + got
            total = total + jnp.sum(jnp.where(hit, picked, 0.0), axis=0, keepdims=True)
        return total

    for one, two, target in ((p1, p2, synth), (q1, q2, born)):
        if rounds > 0 and target is synth:
            target[steps - 2 : steps, :] = one[...]
            continue
        first = [
            one[4 : 4 + size_x, half, 8 : 8 + size_y, :].reshape(rows, LANES) for half in range(2)
        ]
        target[steps - 2 : steps - 1, :] = at(first)
        second = [part.reshape(rows, LANES) for part in halves(two[...])]
        target[steps - 1 : steps, :] = at(second)


    if rounds > 0:
        for k in range(rounds):
            synth[2 * k : 2 * k + 2, :] = earlier[2 * k][...]
            born[2 * k : 2 * k + 2, :] = earlier[2 * k + 1][...]
        residual = observed[...] - synth[...]
        tangent = born[...]
        synth[...] = residual
        numer, denom = jnp.sum(residual * tangent), jnp.sum(tangent * tangent)
        lane = lax.broadcasted_iota(jnp.int32, spread.shape, 2)
        spread[...] = jnp.where(lane == 0, numer, jnp.where(lane == 1, denom, 0.0))


def receive(cells, p1, p2, q1, q2, earlier=(), observed=None, total=0):
    count = cells.shape[1]
    rounds = len(earlier) // 2 if total else (-1 if observed is None else 0)
    outs = [struct(2 * max(rounds, 0) + 2, count)] * 2
    args = [cells, p1, p2, q1, q2]
    if rounds == 0:
        outs.append(struct(*observed.shape))
        args.append(observed)
    elif rounds > 0:
        outs.append(struct(total, 1, LANES))
        args += [*earlier, observed]
    return pl.pallas_call(
        functools.partial(receive_kernel, rounds),
        out_shape=outs,
        in_specs=[VMEM] * len(args),
        out_specs=[VMEM] * len(outs),
        compiler_params=params(),
        cost_estimate=cost(20_000_000, 2_500_000),
        name="receive",
    )(*args)


def finish_kernel(sums, residual, born, speed, smooth, predicted, model, traces, field, sems):
    lane = lax.broadcasted_iota(jnp.int32, sums.shape, 2)
    values = sums[...]
    numer = jnp.sum(jnp.where(lane == 0, values, 0.0))
    denom = jnp.sum(jnp.where(lane == 1, values, 0.0))
    length = jnp.full((1, LANES), numer) / (jnp.full((1, LANES), denom) + 1e-6)
    traces[...] = residual[...] - length * born[...]
    first = pltpu.make_async_copy(traces, predicted, sems.at[0])
    first.start()
    both = jnp.concatenate([length, length], axis=1)
    field[...] = speed[...] + both[None] * smooth[...]
    second = pltpu.make_async_copy(field, model, sems.at[1])
    second.start()
    first.wait()
    second.wait()


def finish(sums, residual, born, speed, smooth):
    outs = [struct(*born.shape), struct(*speed.shape)]
    return pl.pallas_call(
        finish_kernel,
        out_shape=outs,
        in_specs=[VMEM] * 5,
        out_specs=[pl.BlockSpec(memory_space=pl.ANY)] * 2,
        scratch_shapes=[
            pltpu.VMEM(born.shape, F32),
            pltpu.VMEM(speed.shape, F32),
            pltpu.SemaphoreType.DMA((2,)),
        ],
        compiler_params=params(),
        cost_estimate=cost(200_000, 800_000),
        name="finish",
    )(sums, residual, born, speed, smooth)


def smooth_kernel(perturb, p_in, q_in, smooth, p_out, q_out, sems):
    copies = [
        pltpu.make_async_copy(p_in, p_out, sems.at[0]),
        pltpu.make_async_copy(q_in, q_out, sems.at[1]),
    ]
    for copy in copies:
        copy.start()
    size_x, size_y, _ = smooth.shape
    lane = lax.broadcasted_iota(jnp.int32, (size_y, LANES), 1)

    def layer_step(layer, carry):
        parts = []
        for half in range(2):

            def along_x(start, half=half):
                span = slice(start, start + size_y)
                return (
                    0.25 * perturb[layer + 3, half, span, :]
                    + 0.5 * perturb[layer + 4, half, span, :]
                    + 0.25 * perturb[layer + 5, half, span, :]
                )

            parts.append(0.25 * along_x(7) + 0.5 * along_x(8) + 0.25 * along_x(9))
        up = [pltpu.roll(value, LANES - 1, 1) for value in parts]
        down = [pltpu.roll(value, 1, 1) for value in parts]
        keep_up, keep_down = lane < LANES - 1, lane >= 1
        above = [jnp.where(keep_up, up[0], up[1]), jnp.where(keep_up, up[1], 0.0)]
        below = [jnp.where(keep_down, down[0], 0.0), jnp.where(keep_down, down[1], down[0])]
        for half in range(2):
            value = 0.25 * below[half] + 0.5 * parts[half] + 0.25 * above[half]
            smooth[layer, :, half * LANES : (half + 1) * LANES] = value
        return carry

    lax.fori_loop(0, size_x, layer_step, 0)
    for copy in copies:
        copy.wait()


def smoothed(shape, perturb, p_now, q_now):
    return pl.pallas_call(
        smooth_kernel,
        out_shape=[struct(*shape)] * 3,
        in_specs=[VMEM] * 3,
        out_specs=[VMEM] + [pl.BlockSpec(memory_space=pl.ANY)] * 2,
        scratch_shapes=[pltpu.SemaphoreType.DMA((2,))],
        compiler_params=params(),
        cost_estimate=cost(1_000_000, 2_200_000),
        name="smooth",
    )(perturb, p_now, q_now)


def on_device(
    pressure_prev, pressure_now, courant, perturbation, source_pos, wavelet, rec_cells, observed
):
    shape = pressure_now.shape
    size_x, size_y, size_z = shape
    count_x, count_y = lax.axis_size("gx"), lax.axis_size("gy")
    steps = wavelet.shape[0]
    near_x, far_x = near_pairs(count_x), far_pairs(count_x)
    pairs_y = [near_pairs(count_y)]
    if count_y > 2:
        pairs_y.append(far_pairs(count_y))
    count = len(pairs_y)
    far_diagonal = [diagonal(far_x, pairs, count_y) for pairs in pairs_y]

    def swap_near(value):
        return lax.ppermute(value, "gx", near_x)

    def swap_far(value):
        return lax.ppermute(value, "gx", far_x)

    def swap_strips(strips, corners):
        got = [lax.ppermute(value, "gy", pairs) for value, pairs in zip(strips, pairs_y)]
        got_corners = [
            lax.ppermute(value, AXES, pairs) for value, pairs in zip(corners, far_diagonal)
        ]
        return got, [swap_near(value) for value in got], got_corners

    p_far, p_near = swap_far(pressure_now), swap_near(pressure_now)
    far_send, near_send, strips, corners = pack(
        shape, count, pressure_now, pressure_prev, courant, perturbation
    )
    far, near = swap_far(far_send), swap_near(near_send)
    strips, near_strips, corners = swap_strips(strips, corners)
    p_prev, speed, perturb = gather_ring(
        shape,
        count,
        (pressure_prev, courant, perturbation),
        near,
        far,
        strips,
        near_strips,
        corners,
    )
    cells = rec_cells.reshape(1, -1)
    p_cur, q_cur, q_prev = pressure_now, None, None
    q_far = q_near = None
    earlier = []
    traces = observed.reshape(steps, -1)
    for step in range(0, steps, 2):
        last = step + 2 >= steps
        sends = 0 if last else count
        around = (strips, near_strips, corners)
        p_pieces = (p_cur, p_near, p_far) + around
        q_pieces = None if q_cur is None else (q_cur, q_near, q_far) + around + (earlier[-1],)
        p_prev, p_cur, drive1, drive2, p_strips = pressure_steps(
            shape, count, sends, step, source_pos, wavelet, p_pieces, p_prev, speed, perturb
        )
        if not last:
            p_far, p_near = swap_far(p_cur), swap_near(p_cur)
        q_prev, q_cur, strips, corners = tangent_steps(
            shape, count, sends, q_pieces, q_prev, speed, drive1, drive2, p_strips
        )
        if not last:
            strips, near_strips, corners = swap_strips(strips, corners)
            q_far, q_near = swap_far(q_cur), swap_near(q_cur)
        if last:
            ready = receive(cells, p_prev, p_cur, p_prev, p_cur)[0]
        if not last:
            got = list(receive(cells, p_prev, p_cur, q_prev, q_cur, (), traces))
            if step == 0:
                held = got.pop()
            traces = None
            earlier += got
    total = count_x * count_y
    residual, born, spread = receive(
        cells, ready, ready, q_prev, q_cur, earlier, held, total
    )
    sums = lax.all_to_all(spread, AXES, 0, 0)
    smooth, p_cur, q_cur = smoothed(shape, perturb, p_cur, q_cur)
    predicted, updated_model = finish(sums, residual, born, courant, smooth)
    predicted = predicted.reshape(observed.shape)
    return (p_cur, q_cur, predicted, updated_model)


def solution(mesh):
    field = P("gx", "gy", None)
    traces = P("gx", "gy", None, None)
    return jax.shard_map(
        on_device,
        mesh=mesh,
        in_specs=(field, field, field, field, P(), P(), field, traces),
        out_specs=(field, field, traces, field),
        check_vma=False,
    )
```
